512 devices in a mesh: pipe: 16 (over y_lo, x, core), ep: 32 (over y_hi, z).
Axes of the slice: x: 4, y: 4 (y_hi: 2, y_lo: 2; y = y_hi * 2 + y_lo), z: 16, core: 2. Of those that a mesh axis runs over, the one named last changes fastest.
Arguments:
- tokens: bfloat16 [4096, 7168], P('ep'), may hold values from -6 to 6
- norm_gain: float32 [7168], replicated, may hold values from 0.1 to 1.9
- router: bfloat16 [7168, 256], P('pipe'), may hold values from -0.0625 to 0.0625
- routes: int32 [4096, 8], P('ep'), may hold values from 0 to 255, all different within a row; in each aligned block of 128 rows (0 to 127, 128 to 255, ...) at most 8 rows name the same one
- w_gate_up: bfloat16 [32, 7168, 2048], P('ep', None, 'pipe'), may hold values from -0.0625 to 0.0625
- w_down: bfloat16 [32, 1024, 7168], P('ep', 'pipe'), may hold values from -0.25 to 0.25
Outputs:
- mixed: bfloat16 [4096, 7168], P('ep', 'pipe')
The draws below stay inside these ranges and needn't reach their ends.
Inputs may be any that keep to these rules, and one draw needn't show every extreme that they name: `routes`: each row names 8 different experts. Among the rows of one index of ep (aligned blocks of 128 rows) no expert is named more than 8 times, a bound that some block reaches.
All inputs are finite; a program needn't handle non-finite values.
Results may differ from the reference program's by a relative error of at most 0.011.
Values may be sent and summed in bfloat16 or wider, within the bound.
A program may use at most 128 MiB of HBM per device.

```python
import math
import jax
import jax.numpy as jnp
import numpy as np
from jax import lax

D = 7168
EXP_FF = 1024
EXPERTS_ALL = 256
TOPK = 8
TOK_DEV = 128
EXPERTS = 32
GROUP = 64
CAP = 8
TOKENS = 4096
N_PIPE = 16
N_EP = 32


def strengthened(result, key, source, target, blocks, factor):
    owner, partner = [(jnp.arange(result.shape[axis_at]) // (result.shape[axis_at] // blocks)).reshape([-1 if axis == axis_at else 1 for axis in range(result.ndim)]) for axis_at in (source, target)]
    chosen = jax.random.permutation(key, blocks)[partner]
    strong = (owner == chosen) | (owner == (partner + blocks // 2) % blocks)
    return jnp.where(strong, factor * result, result)


def shard_levels(stream_key, extent, pieces, least, largest):
    def one(position, blocks):
        heights = jax.random.uniform(jax.random.fold_in(jax.random.fold_in(stream_key, 6), position), (blocks,), jnp.float32, least / len(pieces), largest / len(pieces))
        return jnp.repeat(jnp.exp(heights), extent[position] // blocks).reshape((-1,) + (1,) * (len(extent) - position - 1))

    gain = one(*pieces[0])
    for cut in pieces[1:]:
        gain = gain * one(*cut)
    return gain


def shared_out(key, own, number, rows, amount, top, most, skew):
    order = jax.random.permutation(key, amount)
    crowded, ordinary = shares(amount, rows * top, most, skew, True), shares(amount, rows * top, most, skew, False)
    places = jnp.arange(amount)

    def named(tallies, rotation):
        used = int((tallies > 0).sum())
        fixed = max(1, used // 4)
        moved = fixed + (places - fixed + rotation * (used - fixed)) % max(1, amount - fixed)
        return jnp.zeros((amount,), jnp.int32).at[order[jnp.where(places < fixed, places, moved)]].set(jnp.asarray(tallies, jnp.int32))

    tallies = jnp.where(number % 4 == 0, named(crowded, number // 4), named(ordinary, number - number // 4 - 1))
    mixed = jax.random.permutation(jax.random.fold_in(own, 3), amount)
    source_of, sink = mixed[0:amount // 2 * 2:2], mixed[1:amount // 2 * 2:2]
    slack = jnp.minimum(tallies[source_of] - 1, most - tallies[sink]) // 2
    slack = jnp.where((source_of == order[0]) | (sink == order[0]) | (tallies[sink] == 0), 0, jnp.maximum(slack, 0))
    moved = jax.random.randint(jax.random.fold_in(own, 4), (amount // 2,), 0, 1 << 20) % (slack + 1)
    tallies = tallies.at[source_of].add(-moved).at[sink].add(moved)
    members = jnp.searchsorted(jnp.cumsum(tallies), jnp.arange(rows * top), side="right").astype(jnp.int32)
    listing = members.reshape(top, rows).T
    listing = listing[jax.random.permutation(jax.random.fold_in(own, 1), rows)]
    rotation = jax.random.randint(jax.random.fold_in(own, 2), (rows, 1), 0, top)
    return jnp.take_along_axis(listing, (jnp.arange(top)[None, :] + rotation) % top, axis=1)


def shares(count, total, reach, lean, full):
    weights = [(1 << 20) // math.isqrt(grade ** lean) + 1 for grade in range(1, count + 1)]
    largest = reach if full else min(reach, max(-(-total // count), total * weights[0] // sum(weights)))
    least = 1 if total - largest >= count - 1 else 0
    given, surplus = [largest] + [least] * (count - 1), total - largest - least * (count - 1)
    while surplus > 0:
        movable = [i for i in range(1, count) if given[i] < largest] or [i for i in range(1, count) if given[i] < reach]
        mass, left = sum([weights[i] for i in movable]), surplus
        for i in movable:
            extra = min(reach - given[i], max(1, left * weights[i] // mass), surplus)
            given[i] = given[i] + extra
            surplus = surplus - extra
    return np.array(given)


def noise(stream_key, extent, scale, most, pieces=(), kind=jnp.bfloat16):
    result = scale * jax.random.normal(stream_key, extent, jnp.float32)
    if pieces:
        result = result * shard_levels(stream_key, extent, pieces, -0.22, 0.18)
    return jnp.clip(result, -most, most).astype(kind)


def gaussian_with(own_key, shape, width, most, shards, heavy, kind=jnp.bfloat16):
    result = width * jax.random.normal(own_key, shape, jnp.float32)
    if shards:
        result = result * shard_levels(own_key, shape, shards, -0.22, 0.18)
    return jnp.clip(strengthened(result, jax.random.fold_in(own_key, 3), *heavy), -most, most).astype(kind)


def setup_inputs(seed: int = 0) -> dict:
    splits = jax.random.split(jax.random.key(seed), 7)
    tokens = noise(splits[0], (TOKENS, D), 1.0, 6.0, ((0, 32),))
    norm_gain = jnp.clip(1.0 + 0.18 * jax.random.normal(splits[1], (D,), jnp.float32), 0.1, 1.9)
    router = noise(splits[2], (D, EXPERTS_ALL), D ** -0.5, 0.0625, ((0, 16),))
    routes_keys = jax.random.split(jax.random.fold_in(splits[3], 1), TOKENS // TOK_DEV)
    routes_turns = jax.random.permutation(jax.random.fold_in(splits[3], 3), TOKENS // TOK_DEV)
    routes = jax.vmap(lambda own, number: shared_out(jax.random.fold_in(splits[3], 2), own, number, TOK_DEV, EXPERTS_ALL, TOPK, CAP, 2))(routes_keys, routes_turns).reshape((TOKENS, TOPK))
    w_gate_up = noise(splits[4], (EXPERTS, D, 2 * EXP_FF), D ** -0.5, 0.0625, ((0, 32), (2, 16)))
    w_down = gaussian_with(splits[5], (EXPERTS, EXP_FF, D), EXP_FF ** -0.5, 0.25, ((0, 32), (1, 16)), (1, 2, 16, 2.0))
    return {"tokens": tokens, "norm_gain": norm_gain, "router": router, "routes": routes, "w_gate_up": w_gate_up, "w_down": w_down}


def reference(tokens, norm_gain, router, routes, w_gate_up, w_down):
    values = tokens.astype(jnp.float32)
    scale = lax.rsqrt(lax.optimization_barrier(jnp.mean(values * values, axis=1, keepdims=True)) + 1e-06)
    normed = (values * scale * norm_gain).astype(jnp.bfloat16)
    affinity = jax.nn.sigmoid(jnp.dot(normed, router, preferred_element_type=jnp.float32))
    picked = jnp.take_along_axis(affinity, routes, axis=1)
    route_weight = 2.5 * picked / lax.optimization_barrier(jnp.sum(picked, axis=1, keepdims=True))
    blocks = routes.reshape(N_EP, TOK_DEV * TOPK)
    onehot = (blocks[:, :, None] == jnp.arange(EXPERTS, dtype=jnp.int32)[None, None, :]).astype(jnp.int32)
    ranks = jnp.cumsum(onehot, axis=1) - 1
    slots = lax.optimization_barrier(jnp.sum(onehot * ranks, axis=2)).astype(jnp.int32)
    owner = jnp.arange(N_EP, dtype=jnp.int32)[:, None]
    flat_routes = routes.reshape(-1)
    sentinel = EXPERTS * N_EP * CAP
    place = jnp.where(flat_routes < EXPERTS, flat_routes * (N_EP * CAP) + (owner * CAP + slots).reshape(-1), sentinel).astype(jnp.int32)
    token_index = (jnp.arange(TOKENS * TOPK, dtype=jnp.int32) // TOPK).astype(jnp.int32)
    source = jnp.full((sentinel + 1,), TOKENS, dtype=jnp.int32).at[place].set(token_index)[:sentinel]
    slot_weight = jnp.zeros((sentinel + 1,), dtype=jnp.float32).at[place].set(route_weight.reshape(-1))[:sentinel]
    padded = jnp.concatenate([normed, jnp.zeros((1, D), dtype=jnp.bfloat16)], axis=0)
    count = N_EP * CAP

    def per_expert(total, expert):
        index = lax.dynamic_slice_in_dim(source, expert * count, count).astype(jnp.int32)
        weight = lax.dynamic_slice_in_dim(slot_weight, expert * count, count)
        inputs = padded[index]
        pair = lax.dynamic_index_in_dim(w_gate_up, expert, 0, keepdims=False).reshape(D, N_PIPE, 2, GROUP)
        down = lax.dynamic_index_in_dim(w_down, expert, 0, keepdims=False)
        gate = jnp.dot(inputs, pair[:, :, 0, :].reshape(D, EXP_FF), preferred_element_type=jnp.float32)
        upper = jnp.dot(inputs, pair[:, :, 1, :].reshape(D, EXP_FF), preferred_element_type=jnp.float32)
        hidden = (jax.nn.silu(gate) * upper).astype(jnp.bfloat16)

        def group_term(step, summed):
            part = lax.dynamic_slice_in_dim(hidden, step * GROUP, GROUP, 1)
            rows = lax.dynamic_slice_in_dim(down, step * GROUP, GROUP, 0)
            rounded = lax.optimization_barrier(jnp.dot(part, rows, preferred_element_type=jnp.float32).astype(jnp.bfloat16))
            return summed + rounded.astype(jnp.float32)
        output = lax.fori_loop(0, N_PIPE, group_term, jnp.zeros((count, D), dtype=jnp.float32))
        return (total.at[index].add(weight[:, None] * output), None)
    start = jnp.zeros((TOKENS + 1, D), dtype=jnp.float32)
    total, unused = lax.scan(per_expert, start, jnp.arange(EXPERTS, dtype=jnp.int32))
    return (values + total[:TOKENS]).astype(jnp.bfloat16)
```

```python
import functools

import jax
import jax.numpy as jnp
from jax import lax
from jax.experimental import pallas as pl
from jax.experimental.pallas import tpu as pltpu
from jax.sharding import PartitionSpec as P

CORES = 2
NX = 4
NY = 2
CHIPS = NX * NY
PIPE = CHIPS * CORES
NZ = 16
HALVES = 2
CAP = 8
LANES = 128
MESH = pl.DeviceIdType.MESH


def remote(src, dst, send, recv, pipe, ep):
    return pltpu.make_async_remote_copy(
        src_ref=src,
        dst_ref=dst,
        send_sem=send,
        recv_sem=recv,
        device_id=(pipe, ep),
        device_id_type=MESH,
    )


def one_hot(routes, first, count, width):
    lane = lax.broadcasted_iota(jnp.int32, (routes.shape[0], width), 1)
    expert = first + lane // count
    named = routes[:, 0:1] == expert
    for k in range(1, routes.shape[1]):
        named = named | (routes[:, k : k + 1] == expert)
    return jnp.where(named, 1.0, 0.0), lane


def slot_matrix(routes, first, width):
    named, lane = one_hot(routes, first, CAP, width)
    rows = routes.shape[0]
    above = lax.broadcasted_iota(jnp.int32, (rows, rows), 1) < lax.broadcasted_iota(
        jnp.int32, (rows, rows), 0
    )
    rank = jnp.dot(
        jnp.where(above, 1.0, 0.0).astype(jnp.bfloat16),
        named.astype(jnp.bfloat16),
        preferred_element_type=jnp.float32,
    )
    return jnp.where(rank == (lane % CAP).astype(jnp.float32), named, 0.0)


def kernel(
    tokens_hbm, gain_ref, router_hbm, routes_ref, gate_up_hbm, down_hbm, out_ref,
    tokens, router, gate_up, down,
    outbox, inbox, rows, part, pair_in, summed, sums_in, back_out, back_in,
    score_out, score_in, weight_out, weight_in,
    load_sem, near_sem, out_sem, gather_send, gather_recv, share_send, share_recv,
    pair_send, pair_recv, sum_send, sum_recv, back_sem, back_near,
    score_sem, weight_sem,
):
    pipe, ep = lax.axis_index("pipe"), lax.axis_index("ep")
    core, chip = lax.rem(pipe, CORES), lax.div(pipe, CORES)
    x, y = lax.rem(chip, NX), lax.div(chip, NX)
    z, side = lax.rem(ep, NZ), lax.div(ep, NZ)
    far_side = lax.rem(side + core, HALVES)
    partner = pipe + 1 - 2 * core
    tok, width = tokens.shape
    columns = width // CHIPS
    tiles = columns // LANES
    half = NZ * CAP
    own = columns // CORES

    loads = []
    for number, (src, dst) in enumerate(
        ((tokens_hbm, tokens), (router_hbm, router.at[pl.ds(core * own, own), :]),
         (gate_up_hbm.at[0], gate_up), (down_hbm.at[0], down))
    ):
        if number == 1:
            router[...] = jnp.zeros_like(router)
        loads.append(pltpu.make_async_copy(src, dst, load_sem.at[number]))
        loads[-1].start()

    barrier = pltpu.get_barrier_semaphore()

    def greet_pipe(i, _):
        pl.semaphore_signal(
            barrier, inc=1, device_id=(lax.rem(pipe + i, PIPE), ep), device_id_type=MESH
        )
        return 0

    lax.fori_loop(1, PIPE, greet_pipe, 0)

    def greet_ep(i, _):
        other = lax.rem(z + i, NZ)
        for k in range(CORES):
            pl.semaphore_signal(
                barrier, inc=1,
                device_id=(CORES * chip + k, lax.rem(side + k, HALVES) * NZ + other),
                device_id_type=MESH,
            )
        return 0

    lax.fori_loop(1, NZ, greet_ep, 0)
    pl.semaphore_signal(
        barrier, inc=1,
        device_id=(CORES * chip + 1, (1 - side) * NZ + z), device_id_type=MESH,
    )

    @pl.when(core == 1)
    def _():
        pl.semaphore_signal(barrier, inc=1, device_id=(partner, ep), device_id_type=MESH)

    routes = routes_ref[...]
    mine = slot_matrix(routes, lax.rem(core + side, HALVES) * NZ, half)
    placing = jnp.transpose(mine).astype(jnp.bfloat16)

    loads[0].wait()
    squares = jnp.zeros((tok, LANES), jnp.float32)
    for at in range(width // LANES):
        values = tokens[:, at * LANES : (at + 1) * LANES].astype(jnp.float32)
        squares += values * values
    scale = lax.rsqrt(jnp.sum(squares, axis=1, keepdims=True) / width + 1e-06)
    block = pl.ds(pl.multiple_of(chip * columns, LANES), columns)
    normed = (tokens[:, block].astype(jnp.float32) * scale * gain_ref[:, block]).astype(
        jnp.bfloat16
    )
    placed = jnp.dot(placing, normed, preferred_element_type=jnp.float32)
    pieces = [
        placed[:, at * LANES : (at + 1) * LANES].reshape(NZ, CAP, LANES)
        for at in range(tiles)
    ]
    pieces.append(jnp.zeros((NZ, CAP, LANES), jnp.float32))
    outbox[...] = jnp.concatenate(pieces, axis=1).astype(jnp.bfloat16)

    pl.semaphore_wait(barrier, PIPE - 1 + 2 * NZ - 1 + core)

    def dispatch(i, _):
        other = lax.rem(z + i, NZ)
        remote(
            outbox.at[other], inbox.at[z], out_sem.at[0], out_sem.at[1],
            pipe, far_side * NZ + other,
        ).start()
        return 0

    lax.fori_loop(1, NZ, dispatch, 0)
    near = remote(
        outbox.at[z], inbox.at[z], near_sem.at[0], near_sem.at[1], pipe, far_side * NZ + z
    )

    @pl.when(core == 1)
    def _():
        near.start()

    @pl.when(core == 0)
    def _():
        pltpu.make_async_copy(outbox.at[z], inbox.at[z], near_sem.at[1]).start()

    loads[1].wait()
    scores = jnp.dot(normed, router[...], preferred_element_type=jnp.float32)
    score_out[...] = scores.reshape(score_out.shape)
    score_in[pipe] = score_out[pipe]

    def send_scores(i, _):
        other = lax.rem(pipe + i, PIPE)
        remote(
            score_out.at[other], score_in.at[pipe], score_sem.at[0], score_sem.at[1], other, ep
        ).start()
        return 0

    lax.fori_loop(1, PIPE, send_scores, 0)

    most = pl.ds(0, NZ - 1)
    pltpu.make_async_copy(inbox.at[most], inbox.at[most], out_sem.at[1]).wait()
    pltpu.make_async_copy(inbox.at[0], inbox.at[0], near_sem.at[1]).wait()
    arrived = inbox[...].astype(jnp.float32)
    keep = pl.ds(pl.multiple_of(core * half, half), half)
    give = pl.ds(pl.multiple_of((1 - core) * half, half), half)
    for at in range(tiles):
        rows[chip, keep, at * LANES : (at + 1) * LANES] = (
            arrived[:, at * CAP : (at + 1) * CAP, :].reshape(half, LANES).astype(jnp.bfloat16)
        )

    def chip_at(ry, rx):
        return lax.rem(y + ry, NY) * NX + lax.rem(x + rx, NX)

    relative = [(ry, rx) for rx in (2, 1, 3, 0) for ry in (1, 0) if (ry, rx) != (0, 0)]
    mirror = {(ry, rx): ry * NX + (NX - rx) % NX for ry, rx in relative}

    def gather_to(ry, rx):
        return remote(
            rows.at[chip, keep, :], rows.at[chip, keep, :],
            gather_send.at[ry * NX + rx], gather_recv.at[mirror[ry, rx]],
            CORES * chip_at(ry, rx) + core, ep,
        )

    def share(ry, rx):
        which = chip_at(ry, rx)
        return remote(
            rows.at[which, keep, :], rows.at[which, keep, :],
            share_send.at[ry * NX + rx], share_recv.at[ry * NX + rx], partner, ep,
        )

    for ry, rx in relative:
        gather_to(ry, rx).start()
    share(0, 0).start()

    most_pipe = pl.ds(0, PIPE - 1)
    pltpu.make_async_copy(score_in.at[most_pipe], score_in.at[most_pipe], score_sem.at[1]).wait()
    affinity = jax.nn.sigmoid(jnp.sum(score_in[...], axis=0))
    group = weight_out.shape[0]
    own_routes = routes_ref[pl.ds(pl.multiple_of(pipe * group, group), group), :]
    chosen, _ = one_hot(own_routes, 0, 1, affinity.shape[1])
    fraction = 2.5 * affinity / jnp.sum(chosen * affinity, axis=1, keepdims=True)
    total_slots = HALVES * half
    spread_row = lax.broadcasted_iota(jnp.int32, (affinity.shape[1], total_slots), 0)
    spread_lane = lax.broadcasted_iota(jnp.int32, (affinity.shape[1], total_slots), 1)
    slot_expert = lax.rem(spread_lane // CAP + side * NZ, HALVES * NZ)
    weight_out[...] = jnp.dot(
        fraction, jnp.where(spread_row == slot_expert, 1.0, 0.0),
        preferred_element_type=jnp.float32, precision=lax.Precision.HIGHEST,
    )
    weight_in[pipe] = weight_out[...]

    def send_weights(i, _):
        other = lax.rem(pipe + i, PIPE)
        remote(weight_out, weight_in.at[pipe], weight_sem.at[0], weight_sem.at[1], other, ep).start()
        return 0

    lax.fori_loop(1, PIPE, send_weights, 0)

    loads[2].wait()

    def project(which):
        return jnp.dot(
            rows[which],
            gate_up[pl.ds(pl.multiple_of(which * columns, LANES), columns), :],
            preferred_element_type=jnp.float32,
        )

    order = [(1, 0), (0, 1), (0, 3), (1, 1), (1, 3), (0, 2), (1, 2)]
    share(0, 0).wait_recv()
    both = project(chip)
    for ry, rx in order:
        gather_to(ry, (NX - rx) % NX).wait_recv()
        share(ry, rx).start()
    for ry, rx in order:
        share(ry, rx).wait_recv()
        both += project(chip_at(ry, rx))
    units = down.shape[0]
    gate, upper = both[:, :units], both[:, units:]
    hidden = (gate / (1.0 + jnp.exp(-gate)) * upper).astype(jnp.bfloat16)

    loads[3].wait()

    def to_partner(ry, rx):
        which = chip_at(ry, rx)
        return remote(
            part.at[which, give, :], pair_in.at[which],
            pair_send.at[ry * NX + rx], pair_recv.at[ry * NX + rx], partner, ep,
        )

    def to_owner(ry, rx):
        return remote(
            summed.at[chip_at(ry, rx)], sums_in.at[mirror[ry, rx]],
            sum_send.at[ry * NX + rx], sum_recv.at[mirror[ry, rx]],
            CORES * chip_at(ry, rx) + core, ep,
        )

    outward = relative + [(0, 0)]
    for ry, rx in outward:
        which = chip_at(ry, rx)
        part[which] = jnp.dot(
            hidden, down[:, pl.ds(pl.multiple_of(which * columns, LANES), columns)],
            preferred_element_type=jnp.float32,
        ).astype(jnp.bfloat16)
        to_partner(ry, rx).start()
    for ry, rx in relative:
        which = chip_at(ry, rx)
        to_partner(ry, rx).wait_recv()
        summed[which] = (
            part[which, keep, :].astype(jnp.float32) + pair_in[which].astype(jnp.float32)
        ).astype(jnp.bfloat16)
        to_owner(ry, rx).start()
    to_partner(0, 0).wait_recv()
    result = part[chip, keep, :].astype(jnp.float32) + pair_in[chip].astype(jnp.float32)

    placed_all = slot_matrix(routes, 0, total_slots)
    first = pl.ds(0, half)
    slots_now = jnp.where(
        side == 0, placed_all,
        jnp.concatenate([placed_all[:, half:], placed_all[:, :half]], axis=1),
    )

    for ry, rx in order:
        to_owner(ry, (NX - rx) % NX).wait_recv()
        result += sums_in[ry * NX + rx].astype(jnp.float32)

    for j in range(CORES):
        pieces = []
        for at in range(4):
            low = j * own + at * LANES
            high = min(low + LANES, (j + 1) * own)
            piece = result[:, low:high]
            if high - low < LANES:
                piece = jnp.concatenate(
                    [piece, jnp.zeros((half, LANES - (high - low)), jnp.float32)], axis=1
                )
            pieces.append(piece.reshape(NZ, CAP, LANES))
        back_out[j] = jnp.concatenate(pieces, axis=1).astype(jnp.bfloat16)

    def go_back(i, _):
        other = lax.rem(z + i, NZ)
        for j in range(CORES):
            remote(
                back_out.at[j, other], back_in.at[core, z], back_sem.at[0], back_sem.at[1],
                CORES * chip + j, far_side * NZ + other,
            ).start()
        return 0

    lax.fori_loop(1, NZ, go_back, 0)
    back_one = remote(
        back_out.at[1, z], back_in.at[core, z], back_near.at[1], back_near.at[2 + core],
        CORES * chip + 1, far_side * NZ + z,
    )
    back_zero = remote(
        back_out.at[0, z], back_in.at[core, z], back_near.at[0], back_near.at[2 + core],
        CORES * chip, far_side * NZ + z,
    )
    back_one.start()

    @pl.when(core == 1)
    def _():
        back_zero.start()

    @pl.when(core == 0)
    def _():
        pltpu.make_async_copy(
            back_out.at[0, z], back_in.at[core, z], back_near.at[2 + core]
        ).start()

    pltpu.make_async_copy(
        weight_in.at[most_pipe], weight_in.at[most_pipe], weight_sem.at[1]
    ).wait()
    combining = slots_now * weight_in[...].reshape(tok, total_slots)
    chip_tokens = tokens[:, block].astype(jnp.float32)
    residual = jnp.where(core == 0, chip_tokens[:, :own], chip_tokens[:, own:])

    pltpu.make_async_copy(
        back_in.at[:, most], back_in.at[:, most], back_sem.at[1]
    ).wait()
    for k in range(HALVES):
        pltpu.make_async_copy(back_in.at[k, 0], back_in.at[k, 0], back_near.at[2 + k]).wait()
    returned = back_in[...].astype(jnp.float32)
    returned = jnp.concatenate(
        [
            returned[:, :, at * CAP : (at + 1) * CAP, :].reshape(total_slots, LANES)
            for at in range(4)
        ],
        axis=1,
    )
    mixed = jnp.dot(
        combining, returned, preferred_element_type=jnp.float32, precision=lax.Precision.HIGHEST
    )
    out_ref[...] = (residual + mixed[:, :own]).astype(jnp.bfloat16)

    pltpu.make_async_copy(outbox.at[most], outbox.at[most], out_sem.at[0]).wait()

    @pl.when(core == 1)
    def _():
        near.wait_send()
        back_zero.wait_send()

    back_one.wait_send()
    pltpu.make_async_copy(back_out.at[:, most], back_out.at[:, most], back_sem.at[0]).wait()
    pltpu.make_async_copy(
        score_out.at[most_pipe], score_out.at[most_pipe], score_sem.at[0]
    ).wait()
    pltpu.make_async_copy(
        weight_in.at[most_pipe], weight_in.at[most_pipe], weight_sem.at[0]
    ).wait()
    for ry, rx in relative:
        gather_to(ry, rx).wait_send()
        to_owner(ry, rx).wait_send()
    for ry, rx in outward:
        share(ry, rx).wait_send()
        to_partner(ry, rx).wait_send()


def shards(tokens, norm_gain, router, routes, w_gate_up, w_down):
    tok, width = tokens.shape
    columns = width // CHIPS
    half = NZ * CAP
    units = w_down.shape[1]
    experts = router.shape[1]
    group = tok // PIPE
    bf16, f32 = jnp.bfloat16, jnp.float32
    dma = pltpu.SemaphoreType.DMA
    anywhere = pl.BlockSpec(memory_space=pl.ANY)
    vmem = pl.BlockSpec(memory_space=pltpu.VMEM)
    return pl.pallas_call(
        kernel,
        out_shape=jax.ShapeDtypeStruct((tok, width // PIPE), bf16),
        in_specs=[anywhere, vmem, anywhere, vmem, anywhere, anywhere],
        out_specs=vmem,
        scratch_shapes=[
            pltpu.VMEM((tok, width), bf16),
            pltpu.VMEM((columns, experts), bf16),
            pltpu.VMEM((width, 2 * units), bf16),
            pltpu.VMEM((units, width), bf16),
            pltpu.VMEM((NZ, 64, LANES), bf16),
            pltpu.VMEM((NZ, 64, LANES), bf16),
            pltpu.VMEM((CHIPS, 2 * half, columns), bf16),
            pltpu.VMEM((CHIPS, 2 * half, columns), bf16),
            pltpu.VMEM((CHIPS, half, columns), bf16),
            pltpu.VMEM((CHIPS, half, columns), bf16),
            pltpu.VMEM((CHIPS, half, columns), bf16),
            pltpu.VMEM((CORES, NZ, 32, LANES), bf16),
            pltpu.VMEM((HALVES, NZ, 32, LANES), bf16),
            pltpu.VMEM((PIPE, group, experts), f32),
            pltpu.VMEM((PIPE, group, experts), f32),
            pltpu.VMEM((group, 2 * half), f32),
            pltpu.VMEM((PIPE, group, 2 * half), f32),
            dma((4,)), dma((2,)), dma((2,)),
            dma((CHIPS,)), dma((CHIPS,)), dma((CHIPS,)), dma((CHIPS,)),
            dma((CHIPS,)), dma((CHIPS,)), dma((CHIPS,)), dma((CHIPS,)),
            dma((2,)), dma((4,)), dma((2,)), dma((2,)),
        ],
        compiler_params=pltpu.CompilerParams(
            collective_id=0, has_side_effects=True, vmem_limit_bytes=56 * 1024 * 1024
        ),
        cost_estimate=pl.CostEstimate(
            flops=2_000_000_000, bytes_accessed=8_000_000, transcendentals=100_000
        ),
    )(tokens, norm_gain.reshape(1, width), router, routes, w_gate_up, w_down)


def solution(mesh):
    placed = (
        P("ep", None),
        P(),
        P("pipe", None),
        P("ep", None),
        P("ep", None, "pipe"),
        P("ep", "pipe", None),
    )
    return jax.shard_map(
        shards, mesh=mesh, in_specs=placed, out_specs=P("ep", "pipe"), check_vma=False
    )
```

```python
import functools

import jax
import jax.numpy as jnp
from jax import lax
from jax.experimental import pallas as pl
from jax.experimental.pallas import tpu as pltpu
from jax.sharding import PartitionSpec as P

CORES = 2
NX = 4
NY = 2
CHIPS = NX * NY
PIPE = CHIPS * CORES
NZ = 16
HALVES = 2
CAP = 8
LANES = 128
MESH = pl.DeviceIdType.MESH


def remote(src, dst, send, recv, pipe, ep):
    return pltpu.make_async_remote_copy(
        src_ref=src,
        dst_ref=dst,
        send_sem=send,
        recv_sem=recv,
        device_id=(pipe, ep),
        device_id_type=MESH,
    )


def one_hot(names, first, count, width):
    row = lax.broadcasted_iota(jnp.int32, (width, names.shape[1]), 0)
    expert = first + row // count
    named = names[0:1, :] == expert
    for k in range(1, names.shape[0]):
        named = named | (names[k : k + 1, :] == expert)
    return jnp.where(named, 1.0, 0.0), row


def slot_matrix(names, first, width):
    named, row = one_hot(names, first, CAP, width)
    tok = names.shape[1]
    earlier = lax.broadcasted_iota(jnp.int32, (tok, tok), 0) < lax.broadcasted_iota(
        jnp.int32, (tok, tok), 1
    )
    rank = jnp.dot(
        named.astype(jnp.bfloat16),
        jnp.where(earlier, 1.0, 0.0).astype(jnp.bfloat16),
        preferred_element_type=jnp.float32,
    )
    return jnp.where(rank == (row % CAP).astype(jnp.float32), named, 0.0)


def kernel(
    tokens_hbm, gain_ref, router_hbm, routes_ref, gate_up_hbm, down_hbm, out_ref,
    tokens, router, gate_up, down,
    outbox, inbox, rows, hidden, back_out, back_in,
    score_out, score_in, weight_out, weight_in,
    load_sem, near_sem, out_sem, gather_send, gather_recv, pair_sem,
    down_sem, hidden_send, hidden_recv, back_sem, back_near,
    score_sem, weight_sem,
):
    pipe, ep = lax.axis_index("pipe"), lax.axis_index("ep")
    core, chip = lax.rem(pipe, CORES), lax.div(pipe, CORES)
    x, y = lax.rem(chip, NX), lax.div(chip, NX)
    z, side = lax.rem(ep, NZ), lax.div(ep, NZ)
    far_side = lax.rem(side + core, HALVES)
    partner = pipe + 1 - 2 * core
    tok, width = tokens.shape
    columns = width // CHIPS
    tiles = columns // LANES
    half = NZ * CAP
    own = columns // CORES
    units = down.shape[2]
    total_slots = HALVES * half

    def column_block(which):
        return pl.ds(pl.multiple_of(which * columns, LANES), columns)

    own_lanes = pl.ds(pl.multiple_of(core * 2 * units, LANES), 2 * units)
    loads = []
    for number, (src, dst) in enumerate(
        ((tokens_hbm, tokens), (router_hbm, router.at[pl.ds(core * own, own), :]),
         (gate_up_hbm.at[0], gate_up.at[:, own_lanes]),
         (down_hbm.at[0, :, column_block(chip)], down.at[chip, core]))
    ):
        if number == 1:
            router[...] = jnp.zeros_like(router)
        loads.append(pltpu.make_async_copy(src, dst, load_sem.at[number]))
        loads[-1].start()

    barrier = pltpu.get_barrier_semaphore()

    def greet_pipe(i, _):
        pl.semaphore_signal(
            barrier, inc=1, device_id=(lax.rem(pipe + i, PIPE), ep), device_id_type=MESH
        )
        return 0

    lax.fori_loop(1, PIPE, greet_pipe, 0)

    def greet_ep(i, _):
        other = lax.rem(z + i, NZ)
        for k in range(CORES):
            pl.semaphore_signal(
                barrier, inc=1,
                device_id=(CORES * chip + k, lax.rem(side + k, HALVES) * NZ + other),
                device_id_type=MESH,
            )
        return 0

    lax.fori_loop(1, NZ, greet_ep, 0)
    pl.semaphore_signal(
        barrier, inc=1,
        device_id=(CORES * chip + 1, (1 - side) * NZ + z), device_id_type=MESH,
    )

    @pl.when(core == 1)
    def _():
        pl.semaphore_signal(barrier, inc=1, device_id=(partner, ep), device_id_type=MESH)

    names = routes_ref[...]
    placing = slot_matrix(names, lax.rem(core + side, HALVES) * NZ, half).astype(jnp.bfloat16)

    loads[0].wait()
    squares = jnp.zeros((tok, LANES), jnp.float32)
    for at in range(width // LANES):
        values = tokens[:, at * LANES : (at + 1) * LANES].astype(jnp.float32)
        squares += values * values
    scale = lax.rsqrt(jnp.sum(squares, axis=1, keepdims=True) / width + 1e-06)
    block = column_block(chip)
    normed = (tokens[:, block].astype(jnp.float32) * scale * gain_ref[:, block]).astype(
        jnp.bfloat16
    )
    placed = jnp.dot(placing, normed, preferred_element_type=jnp.float32)
    pieces = [
        placed[:, at * LANES : (at + 1) * LANES].reshape(NZ, CAP, LANES)
        for at in range(tiles)
    ]
    pieces.append(jnp.zeros((NZ, CAP, LANES), jnp.float32))
    outbox[...] = jnp.concatenate(pieces, axis=1).astype(jnp.bfloat16)

    pl.semaphore_wait(barrier, PIPE - 1 + 2 * NZ - 1 + core)

    def dispatch(i, _):
        other = lax.rem(z + i, NZ)
        remote(
            outbox.at[other], inbox.at[z], out_sem.at[0], out_sem.at[1],
            pipe, far_side * NZ + other,
        ).start()
        return 0

    lax.fori_loop(1, NZ, dispatch, 0)
    near = remote(
        outbox.at[z], inbox.at[z], near_sem.at[0], near_sem.at[1], pipe, far_side * NZ + z
    )

    @pl.when(core == 1)
    def _():
        near.start()

    @pl.when(core == 0)
    def _():
        pltpu.make_async_copy(outbox.at[z], inbox.at[z], near_sem.at[1]).start()

    def chip_at(ry, rx):
        return lax.rem(y + ry, NY) * NX + lax.rem(x + rx, NX)

    relative = [(ry, rx) for rx in (2, 1, 3, 0) for ry in (1, 0) if (ry, rx) != (0, 0)]
    mirror = {(ry, rx): ry * NX + (NX - rx) % NX for ry, rx in relative}

    def down_to(ry, rx):
        return remote(
            down_hbm.at[0, :, column_block(chip_at(ry, rx))], down.at[chip, core],
            down_sem.at[ry * NX + rx], down_sem.at[CHIPS + mirror[ry, rx]],
            CORES * chip_at(ry, rx) + core, ep,
        )

    for ry, rx in relative:
        down_to(ry, rx).start()
    gate_up_pair = remote(
        gate_up_hbm.at[0], gate_up.at[:, own_lanes], pair_sem.at[0], pair_sem.at[1], partner, ep
    )
    gate_up_pair.start()

    loads[1].wait()
    scores = jnp.dot(normed, router[...], preferred_element_type=jnp.float32)
    score_out[...] = scores.reshape(score_out.shape)
    score_in[pipe] = score_out[pipe]

    def send_scores(i, _):
        other = lax.rem(pipe + i, PIPE)
        remote(
            score_out.at[other], score_in.at[pipe], score_sem.at[0], score_sem.at[1], other, ep
        ).start()
        return 0

    lax.fori_loop(1, PIPE, send_scores, 0)

    most = pl.ds(0, NZ - 1)
    pltpu.make_async_copy(inbox.at[most], inbox.at[most], out_sem.at[1]).wait()
    pltpu.make_async_copy(inbox.at[0], inbox.at[0], near_sem.at[1]).wait()
    arrived = inbox[...].astype(jnp.float32)
    for at in range(tiles):
        rows[chip, :, at * LANES : (at + 1) * LANES] = (
            arrived[:, at * CAP : (at + 1) * CAP, :].reshape(half, LANES).astype(jnp.bfloat16)
        )

    def gather_to(ry, rx):
        return remote(
            rows.at[chip], rows.at[chip],
            gather_send.at[ry * NX + rx], gather_recv.at[mirror[ry, rx]],
            CORES * chip_at(ry, rx) + core, ep,
        )

    for ry, rx in relative:
        gather_to(ry, rx).start()

    loads[3].wait()
    for ry, rx in relative:
        down_to(ry, rx).wait_recv()
    down_pair = remote(
        down.at[:, core], down.at[:, core], pair_sem.at[2], pair_sem.at[3], partner, ep
    )
    down_pair.start()

    most_pipe = pl.ds(0, PIPE - 1)
    pltpu.make_async_copy(score_in.at[most_pipe], score_in.at[most_pipe], score_sem.at[1]).wait()
    affinity = jax.nn.sigmoid(jnp.sum(score_in[...], axis=0))
    group, experts = affinity.shape
    pick_token = lax.broadcasted_iota(jnp.int32, (group, tok), 1)
    pick_row = lax.broadcasted_iota(jnp.int32, (group, tok), 0)
    pick = jnp.where(pick_token == pick_row + pipe * group, 1.0, 0.0).astype(jnp.bfloat16)
    chosen_all, _ = one_hot(names, 0, 1, experts)
    chosen = lax.dot_general(
        pick, chosen_all.astype(jnp.bfloat16), (((1,), (1,)), ((), ())),
        preferred_element_type=jnp.float32,
    )
    fraction = 2.5 * affinity / jnp.sum(chosen * affinity, axis=1, keepdims=True)
    spread_row = lax.broadcasted_iota(jnp.int32, (experts, total_slots), 0)
    spread_lane = lax.broadcasted_iota(jnp.int32, (experts, total_slots), 1)
    slot_expert = lax.rem(spread_lane // CAP + side * NZ, HALVES * NZ)
    weight_out[...] = jnp.dot(
        fraction, jnp.where(spread_row == slot_expert, 1.0, 0.0),
        preferred_element_type=jnp.float32, precision=lax.Precision.HIGHEST,
    )
    weight_in[pipe] = weight_out[...]

    def send_weights(i, _):
        other = lax.rem(pipe + i, PIPE)
        remote(weight_out, weight_in.at[pipe], weight_sem.at[0], weight_sem.at[1], other, ep).start()
        return 0

    lax.fori_loop(1, PIPE, send_weights, 0)

    loads[2].wait()
    gate_up_pair.wait_recv()

    def project(which):
        return jnp.dot(
            rows[which],
            gate_up[pl.ds(pl.multiple_of(which * columns, LANES), columns), :],
            preferred_element_type=jnp.float32,
        )

    order = [(1, 0), (0, 1), (0, 3), (1, 1), (1, 3), (0, 2), (1, 2)]
    both = project(chip)
    for ry, rx in order:
        gather_to(ry, (NX - rx) % NX).wait_recv()
        both += project(chip_at(ry, rx))
    parts = []
    for k in range(CORES):
        gate = both[:, 2 * k * units : (2 * k + 1) * units]
        upper = both[:, (2 * k + 1) * units : (2 * k + 2) * units]
        parts.append(gate / (1.0 + jnp.exp(-gate)) * upper)
    hidden[chip] = jnp.concatenate(parts, axis=1).astype(jnp.bfloat16)

    def hidden_to(ry, rx):
        return remote(
            hidden.at[chip], hidden.at[chip],
            hidden_send.at[ry * NX + rx], hidden_recv.at[mirror[ry, rx]],
            CORES * chip_at(ry, rx) + core, ep,
        )

    for ry, rx in relative:
        hidden_to(ry, rx).start()

    down_pair.wait_recv()

    def lower(which):
        return jnp.dot(
            hidden[which], down[which].reshape(CORES * units, columns),
            preferred_element_type=jnp.float32,
        )

    result = lower(chip)
    for ry, rx in order:
        hidden_to(ry, (NX - rx) % NX).wait_recv()
        result += lower(chip_at(ry, rx))

    for j in range(CORES):
        pieces = []
        for at in range(4):
            low = j * own + at * LANES
            high = min(low + LANES, (j + 1) * own)
            piece = result[:, low:high]
            if high - low < LANES:
                piece = jnp.concatenate(
                    [piece, jnp.zeros((half, LANES - (high - low)), jnp.float32)], axis=1
                )
            pieces.append(piece.reshape(NZ, CAP, LANES))
        back_out[j] = jnp.concatenate(pieces, axis=1).astype(jnp.bfloat16)

    def go_back(i, _):
        other = lax.rem(z + i, NZ)
        for j in range(CORES):
            remote(
                back_out.at[j, other], back_in.at[core, z], back_sem.at[0], back_sem.at[1],
                CORES * chip + j, far_side * NZ + other,
            ).start()
        return 0

    lax.fori_loop(1, NZ, go_back, 0)
    back_one = remote(
        back_out.at[1, z], back_in.at[core, z], back_near.at[1], back_near.at[2 + core],
        CORES * chip + 1, far_side * NZ + z,
    )
    back_zero = remote(
        back_out.at[0, z], back_in.at[core, z], back_near.at[0], back_near.at[2 + core],
        CORES * chip, far_side * NZ + z,
    )
    back_one.start()

    @pl.when(core == 1)
    def _():
        back_zero.start()

    @pl.when(core == 0)
    def _():
        pltpu.make_async_copy(
            back_out.at[0, z], back_in.at[core, z], back_near.at[2 + core]
        ).start()

    slots_all = slot_matrix(names, 0, total_slots)
    slots_now = jnp.where(
        side == 0, slots_all, jnp.concatenate([slots_all[half:], slots_all[:half]], axis=0)
    )
    pltpu.make_async_copy(
        weight_in.at[most_pipe], weight_in.at[most_pipe], weight_sem.at[1]
    ).wait()
    combining = jnp.transpose(slots_now) * weight_in[...].reshape(tok, total_slots)
    chip_tokens = tokens[:, block].astype(jnp.float32)
    padding = jnp.zeros((tok, 4 * LANES - own), jnp.float32)
    residual = jnp.where(
        core == 0, chip_tokens[:, : 4 * LANES],
        jnp.concatenate([chip_tokens[:, own:], padding], axis=1),
    )

    pltpu.make_async_copy(outbox.at[most], outbox.at[most], out_sem.at[0]).wait()

    @pl.when(core == 1)
    def _():
        near.wait_send()

    pltpu.make_async_copy(
        score_out.at[most_pipe], score_out.at[most_pipe], score_sem.at[0]
    ).wait()
    pltpu.make_async_copy(
        weight_in.at[most_pipe], weight_in.at[most_pipe], weight_sem.at[0]
    ).wait()
    for ry, rx in relative:
        down_to(ry, rx).wait_send()
        gather_to(ry, rx).wait_send()
        hidden_to(ry, rx).wait_send()
    gate_up_pair.wait_send()
    down_pair.wait_send()

    pltpu.make_async_copy(
        back_in.at[:, most], back_in.at[:, most], back_sem.at[1]
    ).wait()
    for k in range(HALVES):
        pltpu.make_async_copy(back_in.at[k, 0], back_in.at[k, 0], back_near.at[2 + k]).wait()
    returned = back_in[...].astype(jnp.float32)
    returned = jnp.concatenate(
        [
            returned[:, :, at * CAP : (at + 1) * CAP, :].reshape(total_slots, LANES)
            for at in range(4)
        ],
        axis=1,
    )
    mixed = residual + jnp.dot(
        combining, returned, preferred_element_type=jnp.float32, precision=lax.Precision.HIGHEST
    )
    out_ref[...] = jnp.transpose(mixed)[:own, :].astype(jnp.bfloat16)

    @pl.when(core == 1)
    def _():
        back_zero.wait_send()

    back_one.wait_send()
    pltpu.make_async_copy(back_out.at[:, most], back_out.at[:, most], back_sem.at[0]).wait()


def shards(tokens, norm_gain, router, routes, w_gate_up, w_down):
    tok, width = tokens.shape
    columns = width // CHIPS
    half = NZ * CAP
    units = w_down.shape[1]
    experts = router.shape[1]
    group = tok // PIPE
    bf16, f32 = jnp.bfloat16, jnp.float32
    dma = pltpu.SemaphoreType.DMA
    anywhere = pl.BlockSpec(memory_space=pl.ANY)
    vmem = pl.BlockSpec(memory_space=pltpu.VMEM)
    mixed = pl.pallas_call(
        kernel,
        out_shape=jax.ShapeDtypeStruct((width // PIPE, tok), bf16),
        in_specs=[anywhere, vmem, anywhere, vmem, anywhere, anywhere],
        out_specs=vmem,
        scratch_shapes=[
            pltpu.VMEM((tok, width), bf16),
            pltpu.VMEM((columns, experts), bf16),
            pltpu.VMEM((width, CORES * 2 * units), bf16),
            pltpu.VMEM((CHIPS, CORES, units, columns), bf16),
            pltpu.VMEM((NZ, 64, LANES), bf16),
            pltpu.VMEM((NZ, 64, LANES), bf16),
            pltpu.VMEM((CHIPS, half, columns), bf16),
            pltpu.VMEM((CHIPS, half, CORES * units), bf16),
            pltpu.VMEM((CORES, NZ, 32, LANES), bf16),
            pltpu.VMEM((HALVES, NZ, 32, LANES), bf16),
            pltpu.VMEM((PIPE, group, experts), f32),
            pltpu.VMEM((PIPE, group, experts), f32),
            pltpu.VMEM((group, 2 * half), f32),
            pltpu.VMEM((PIPE, group, 2 * half), f32),
            dma((4,)), dma((2,)), dma((2,)),
            dma((CHIPS,)), dma((CHIPS,)), dma((4,)),
            dma((2 * CHIPS,)), dma((CHIPS,)), dma((CHIPS,)),
            dma((2,)), dma((4,)), dma((2,)), dma((2,)),
        ],
        compiler_params=pltpu.CompilerParams(
            collective_id=0, has_side_effects=True, vmem_limit_bytes=56 * 1024 * 1024
        ),
        cost_estimate=pl.CostEstimate(
            flops=2_000_000_000, bytes_accessed=8_000_000, transcendentals=100_000
        ),
    )(tokens, norm_gain.reshape(1, width), router, routes.T, w_gate_up, w_down)
    return mixed.T


def solution(mesh):
    placed = (
        P("ep", None),
        P(),
        P("pipe", None),
        P("ep", None),
        P("ep", None, "pipe"),
        P("ep", "pipe", None),
    )
    return jax.shard_map(
        shards, mesh=mesh, in_specs=placed, out_specs=P("ep", "pipe"), check_vma=False
    )
```

```python
import functools

import jax
import jax.numpy as jnp
from jax import lax
from jax.experimental import pallas as pl
from jax.experimental.pallas import tpu as pltpu
from jax.sharding import PartitionSpec as P

CORES = 2
NX = 4
NY = 2
CHIPS = NX * NY
PIPE = CHIPS * CORES
NZ = 16
HALVES = 2
CAP = 8
PARTS = ((0, 4), (4, 3))
PIECE = 32
LANES = 128
MESH = pl.DeviceIdType.MESH


def remote(src, dst, send, recv, pipe, ep):
    return pltpu.make_async_remote_copy(
        src_ref=src,
        dst_ref=dst,
        send_sem=send,
        recv_sem=recv,
        device_id=(pipe, ep),
        device_id_type=MESH,
    )


def one_hot(names, first, count, width):
    row = lax.broadcasted_iota(jnp.int32, (width, names.shape[1]), 0)
    expert = first + row // count
    named = names[0:1, :] == expert
    for k in range(1, names.shape[0]):
        named = named | (names[k : k + 1, :] == expert)
    return jnp.where(named, 1.0, 0.0), row


def slot_matrix(names, first, width):
    named, row = one_hot(names, first, CAP, width)
    tok = names.shape[1]
    earlier = lax.broadcasted_iota(jnp.int32, (tok, tok), 0) < lax.broadcasted_iota(
        jnp.int32, (tok, tok), 1
    )
    rank = jnp.dot(
        named.astype(jnp.bfloat16),
        jnp.where(earlier, 1.0, 0.0).astype(jnp.bfloat16),
        preferred_element_type=jnp.float32,
    )
    return jnp.where(rank == (row % CAP).astype(jnp.float32), named, 0.0)


def kernel(
    tokens_hbm, gain_ref, router_hbm, routes_ref, gate_up_hbm, down_hbm, out_ref,
    tokens, router, gate_up, down,
    outbox, inbox, rows_a, rows_b, hidden, back_out, back_in,
    score_out, score_in, weight_out, weight_in,
    load_sem, near_sem, out_sem, gather_send, gather_recv, pair_sem,
    down_sem, hidden_send, hidden_recv, back_sem, back_near,
    score_sem, weight_sem,
):
    pipe, ep = lax.axis_index("pipe"), lax.axis_index("ep")
    core, chip = lax.rem(pipe, CORES), lax.div(pipe, CORES)
    x, y = lax.rem(chip, NX), lax.div(chip, NX)
    z, side = lax.rem(ep, NZ), lax.div(ep, NZ)
    far_side = lax.rem(side + core, HALVES)
    partner = pipe + 1 - 2 * core
    tok, width = tokens.shape
    columns = width // CHIPS
    tiles = columns // LANES
    half = NZ * CAP
    own = columns // CORES
    units = down.shape[2]
    total_slots = HALVES * half

    def column_block(which):
        return pl.ds(pl.multiple_of(which * columns, LANES), columns)

    own_lanes = pl.ds(pl.multiple_of(core * 2 * units, LANES), 2 * units)
    quarter = width // 4
    token_loads = [
        pltpu.make_async_copy(
            tokens_hbm.at[:, pl.ds(n * quarter, quarter)],
            tokens.at[:, pl.ds(n * quarter, quarter)],
            load_sem.at[3 + n],
        )
        for n in range(4)
    ]
    for load in token_loads:
        load.start()

    barrier = pltpu.get_barrier_semaphore()

    def greet_pipe(i, _):
        pl.semaphore_signal(
            barrier, inc=1, device_id=(lax.rem(pipe + i, PIPE), ep), device_id_type=MESH
        )
        return 0

    lax.fori_loop(1, PIPE, greet_pipe, 0)

    def greet_ep(i, _):
        other = lax.rem(z + i, NZ)
        for k in range(CORES):
            pl.semaphore_signal(
                barrier, inc=1,
                device_id=(CORES * chip + k, lax.rem(side + k, HALVES) * NZ + other),
                device_id_type=MESH,
            )
        return 0

    lax.fori_loop(1, NZ, greet_ep, 0)
    pl.semaphore_signal(
        barrier, inc=1,
        device_id=(CORES * chip + 1, (1 - side) * NZ + z), device_id_type=MESH,
    )

    @pl.when(core == 1)
    def _():
        pl.semaphore_signal(barrier, inc=1, device_id=(partner, ep), device_id_type=MESH)

    names = routes_ref[...]
    placing = slot_matrix(names, lax.rem(core + side, HALVES) * NZ, half).astype(jnp.bfloat16)

    squares = jnp.zeros((tok, LANES), jnp.float32)
    for n in range(4):
        token_loads[n].wait()
        for at in range(n * quarter // LANES, (n + 1) * quarter // LANES):
            values = tokens[:, at * LANES : (at + 1) * LANES].astype(jnp.float32)
            squares += values * values
    router[...] = jnp.zeros_like(router)
    loads = [
        pltpu.make_async_copy(src, dst, load_sem.at[number])
        for number, (src, dst) in enumerate(
            ((router_hbm, router.at[pl.ds(core * own, own), :]),
             (gate_up_hbm.at[0], gate_up.at[:, own_lanes]),
             (down_hbm.at[0, :, column_block(chip)], down.at[chip, core]))
        )
    ]
    for load in loads:
        load.start()
    scale = lax.rsqrt(jnp.sum(squares, axis=1, keepdims=True) / width + 1e-06)
    block = column_block(chip)
    normed = (tokens[:, block].astype(jnp.float32) * scale * gain_ref[:, block]).astype(
        jnp.bfloat16
    )
    placed = jnp.dot(placing, normed, preferred_element_type=jnp.float32)
    for part, (first, count) in enumerate(PARTS):
        pieces = [
            placed[:, at * LANES : (at + 1) * LANES].reshape(NZ, CAP, LANES)
            for at in range(first, first + count)
        ]
        if count < 4:
            pieces.append(jnp.zeros((NZ, PIECE - count * CAP, LANES), jnp.float32))
        outbox[part] = jnp.concatenate(pieces, axis=1).astype(jnp.bfloat16)

    pl.semaphore_wait(barrier, PIPE - 1 + 2 * NZ - 1 + core)

    near = []
    for part in range(2):
        def dispatch(i, _):
            other = lax.rem(z + i, NZ)
            remote(
                outbox.at[part, other], inbox.at[part, z],
                out_sem.at[2 * part], out_sem.at[2 * part + 1],
                pipe, far_side * NZ + other,
            ).start()
            return 0

        lax.fori_loop(1, NZ, dispatch, 0)
        near.append(remote(
            outbox.at[part, z], inbox.at[part, z],
            near_sem.at[2 * part], near_sem.at[2 * part + 1], pipe, far_side * NZ + z,
        ))

    @pl.when(core == 1)
    def _():
        for copy in near:
            copy.start()

    @pl.when(core == 0)
    def _():
        for part in range(2):
            pltpu.make_async_copy(
                outbox.at[part, z], inbox.at[part, z], near_sem.at[2 * part + 1]
            ).start()

    def chip_at(ry, rx):
        return lax.rem(y + ry, NY) * NX + lax.rem(x + rx, NX)

    relative = [(ry, rx) for rx in (2, 1, 3, 0) for ry in (1, 0) if (ry, rx) != (0, 0)]
    mirror = {(ry, rx): ry * NX + (NX - rx) % NX for ry, rx in relative}

    def down_to(ry, rx):
        return remote(
            down_hbm.at[0, :, column_block(chip_at(ry, rx))], down.at[chip, core],
            down_sem.at[ry * NX + rx], down_sem.at[CHIPS + mirror[ry, rx]],
            CORES * chip_at(ry, rx) + core, ep,
        )

    for ry, rx in relative:
        down_to(ry, rx).start()
    gate_up_pair = remote(
        gate_up_hbm.at[0], gate_up.at[:, own_lanes], pair_sem.at[0], pair_sem.at[1], partner, ep
    )
    gate_up_pair.start()

    loads[0].wait()
    scores = jnp.dot(normed, router[...], preferred_element_type=jnp.float32)
    score_out[...] = scores.reshape(score_out.shape)
    score_in[pipe] = score_out[pipe]

    def send_scores(i, _):
        other = lax.rem(pipe + i, PIPE)
        remote(
            score_out.at[other], score_in.at[pipe], score_sem.at[0], score_sem.at[1], other, ep
        ).start()
        return 0

    lax.fori_loop(1, PIPE, send_scores, 0)

    most = pl.ds(0, NZ - 1)
    gathered = (rows_a, rows_b)
    sent = []

    def arrive(part):
        first, count = PARTS[part]
        pltpu.make_async_copy(
            inbox.at[part, most], inbox.at[part, most], out_sem.at[2 * part + 1]
        ).wait()
        pltpu.make_async_copy(
            inbox.at[part, 0], inbox.at[part, 0], near_sem.at[2 * part + 1]
        ).wait()
        arrived = inbox[part].astype(jnp.float32)
        for at in range(count):
            gathered[part][chip, :, at * LANES : (at + 1) * LANES] = (
                arrived[:, at * CAP : (at + 1) * CAP, :].reshape(half, LANES).astype(jnp.bfloat16)
            )

    def block_ref(part, ry, rx, piece):
        ref = gathered[part].at[chip_at(ry, rx)]
        return ref if piece is None else ref.at[pl.ds(piece * (half // 2), half // 2), :]

    def recv_sem(part, ry, rx, piece):
        return gather_recv.at[(part * CHIPS + (ry % NY) * NX + rx % NX) * 2 + (piece or 0)]

    def pass_on(part, block, target, piece=None):
        (ry, rx), (ty, tx) = block, target
        ref = block_ref(part, ry, rx, piece)
        copy = remote(
            ref, ref, gather_send.at[len(sent)], recv_sem(part, ry + ty, rx - tx + NX, piece),
            CORES * chip_at(ty, tx) + core, ep,
        )
        copy.start()
        sent.append(copy)

    def take(part, ry, rx, piece=None):
        ref = block_ref(part, ry, rx, piece)
        pltpu.make_async_copy(ref, ref, recv_sem(part, ry, rx, piece)).wait()

    up, plus, minus = (1, 0), (0, 1), (0, 3)

    arrive(0)
    for target in (plus, minus, up):
        pass_on(0, (0, 0), target)

    take(0, 1, 0)
    pass_on(0, (1, 0), plus)
    pass_on(0, (1, 0), minus)
    for ry in range(NY):
        take(0, ry, 3)
        pass_on(0, (ry, 3), plus, 0)
        take(0, ry, 1)
        pass_on(0, (ry, 1), minus, 1)

    arrive(1)
    for target in (plus, minus, up):
        pass_on(1, (0, 0), target)

    loads[2].wait()
    for ry, rx in relative:
        down_to(ry, rx).wait_recv()
    down_pair = remote(
        down.at[:, core], down.at[:, core], pair_sem.at[2], pair_sem.at[3], partner, ep
    )
    down_pair.start()

    most_pipe = pl.ds(0, PIPE - 1)
    pltpu.make_async_copy(score_in.at[most_pipe], score_in.at[most_pipe], score_sem.at[1]).wait()
    affinity = jax.nn.sigmoid(jnp.sum(score_in[...], axis=0))
    group, experts = affinity.shape
    pick_token = lax.broadcasted_iota(jnp.int32, (group, tok), 1)
    pick_row = lax.broadcasted_iota(jnp.int32, (group, tok), 0)
    pick = jnp.where(pick_token == pick_row + pipe * group, 1.0, 0.0).astype(jnp.bfloat16)
    chosen_all, _ = one_hot(names, 0, 1, experts)
    chosen = lax.dot_general(
        pick, chosen_all.astype(jnp.bfloat16), (((1,), (1,)), ((), ())),
        preferred_element_type=jnp.float32,
    )
    fraction = 2.5 * affinity / jnp.sum(chosen * affinity, axis=1, keepdims=True)
    spread_row = lax.broadcasted_iota(jnp.int32, (experts, total_slots), 0)
    spread_lane = lax.broadcasted_iota(jnp.int32, (experts, total_slots), 1)
    slot_expert = lax.rem(spread_lane // CAP + side * NZ, HALVES * NZ)
    weight_out[...] = jnp.dot(
        fraction, jnp.where(spread_row == slot_expert, 1.0, 0.0),
        preferred_element_type=jnp.float32, precision=lax.Precision.HIGHEST,
    )
    weight_in[pipe] = weight_out[...]

    def send_weights(i, _):
        other = lax.rem(pipe + i, PIPE)
        remote(weight_out, weight_in.at[pipe], weight_sem.at[0], weight_sem.at[1], other, ep).start()
        return 0

    lax.fori_loop(1, PIPE, send_weights, 0)

    loads[1].wait()
    gate_up_pair.wait_recv()

    def project(part, ry, rx):
        first, count = PARTS[part]
        which = chip_at(ry, rx)
        start = pl.multiple_of(which * columns + first * LANES, LANES)
        return jnp.dot(
            gathered[part][which], gate_up[pl.ds(start, count * LANES), :],
            preferred_element_type=jnp.float32,
        )

    both = project(0, 0, 0) + project(0, 1, 0)
    take(1, 0, 3)
    pass_on(1, (0, 3), plus, 0)
    pass_on(1, (0, 3), up)
    take(1, 0, 1)
    pass_on(1, (0, 1), minus, 1)
    pass_on(1, (0, 1), up)
    for ry in range(NY):
        both += project(0, ry, 3) + project(0, ry, 1)
    for piece in range(2):
        take(1, 0, 2, piece)
        pass_on(1, (0, 2), up, piece)
    both += project(1, 0, 0) + project(1, 0, 1) + project(1, 0, 2) + project(1, 0, 3)
    for ry in range(NY):
        for piece in range(2):
            take(0, ry, 2, piece)
        both += project(0, ry, 2)
    for rx in (0, 3, 1):
        take(1, 1, rx)
        both += project(1, 1, rx)
    for piece in range(2):
        take(1, 1, 2, piece)
    both += project(1, 1, 2)
    parts = []
    for k in range(CORES):
        gate = both[:, 2 * k * units : (2 * k + 1) * units]
        upper = both[:, (2 * k + 1) * units : (2 * k + 2) * units]
        parts.append(gate / (1.0 + jnp.exp(-gate)) * upper)
    hidden[chip] = jnp.concatenate(parts, axis=1).astype(jnp.bfloat16)

    def hidden_to(ry, rx):
        return remote(
            hidden.at[chip], hidden.at[chip],
            hidden_send.at[ry * NX + rx], hidden_recv.at[mirror[ry, rx]],
            CORES * chip_at(ry, rx) + core, ep,
        )

    for ry, rx in relative:
        hidden_to(ry, rx).start()

    down_pair.wait_recv()

    def lower(which):
        return jnp.dot(
            hidden[which], down[which].reshape(CORES * units, columns),
            preferred_element_type=jnp.float32,
        )

    order = [(1, 0), (0, 1), (0, 3), (1, 1), (1, 3), (0, 2), (1, 2)]
    result = lower(chip)
    for ry, rx in order:
        hidden_to(ry, (NX - rx) % NX).wait_recv()
        result += lower(chip_at(ry, rx))

    for j in range(CORES):
        pieces = []
        for at in range(4):
            low = j * own + at * LANES
            high = min(low + LANES, (j + 1) * own)
            piece = result[:, low:high]
            if high - low < LANES:
                piece = jnp.concatenate(
                    [piece, jnp.zeros((half, LANES - (high - low)), jnp.float32)], axis=1
                )
            pieces.append(piece.reshape(NZ, CAP, LANES))
        back_out[j] = jnp.concatenate(pieces, axis=1).astype(jnp.bfloat16)

    def go_back(i, _):
        other = lax.rem(z + i, NZ)
        for j in range(CORES):
            remote(
                back_out.at[j, other], back_in.at[core, z], back_sem.at[0], back_sem.at[1],
                CORES * chip + j, far_side * NZ + other,
            ).start()
        return 0

    lax.fori_loop(1, NZ, go_back, 0)
    back_one = remote(
        back_out.at[1, z], back_in.at[core, z], back_near.at[1], back_near.at[2 + core],
        CORES * chip + 1, far_side * NZ + z,
    )
    back_zero = remote(
        back_out.at[0, z], back_in.at[core, z], back_near.at[0], back_near.at[2 + core],
        CORES * chip, far_side * NZ + z,
    )
    back_one.start()

    @pl.when(core == 1)
    def _():
        back_zero.start()

    @pl.when(core == 0)
    def _():
        pltpu.make_async_copy(
            back_out.at[0, z], back_in.at[core, z], back_near.at[2 + core]
        ).start()

    slots_all = slot_matrix(names, 0, total_slots)
    slots_now = jnp.where(
        side == 0, slots_all, jnp.concatenate([slots_all[half:], slots_all[:half]], axis=0)
    )
    pltpu.make_async_copy(
        weight_in.at[most_pipe], weight_in.at[most_pipe], weight_sem.at[1]
    ).wait()
    combining = jnp.transpose(slots_now) * weight_in[...].reshape(tok, total_slots)
    chip_tokens = tokens[:, block].astype(jnp.float32)
    padding = jnp.zeros((tok, 4 * LANES - own), jnp.float32)
    residual = jnp.where(
        core == 0, chip_tokens[:, : 4 * LANES],
        jnp.concatenate([chip_tokens[:, own:], padding], axis=1),
    )

    for part in range(2):
        pltpu.make_async_copy(
            outbox.at[part, most], outbox.at[part, most], out_sem.at[2 * part]
        ).wait()

    @pl.when(core == 1)
    def _():
        for copy in near:
            copy.wait_send()

    pltpu.make_async_copy(
        score_out.at[most_pipe], score_out.at[most_pipe], score_sem.at[0]
    ).wait()
    pltpu.make_async_copy(
        weight_in.at[most_pipe], weight_in.at[most_pipe], weight_sem.at[0]
    ).wait()
    for ry, rx in relative:
        down_to(ry, rx).wait_send()
        hidden_to(ry, rx).wait_send()
    for copy in sent:
        copy.wait_send()
    gate_up_pair.wait_send()
    down_pair.wait_send()

    pltpu.make_async_copy(
        back_in.at[:, most], back_in.at[:, most], back_sem.at[1]
    ).wait()
    for k in range(HALVES):
        pltpu.make_async_copy(back_in.at[k, 0], back_in.at[k, 0], back_near.at[2 + k]).wait()
    returned = back_in[...].astype(jnp.float32)
    returned = jnp.concatenate(
        [
            returned[:, :, at * CAP : (at + 1) * CAP, :].reshape(total_slots, LANES)
            for at in range(4)
        ],
        axis=1,
    )
    mixed = residual + jnp.dot(
        combining, returned, preferred_element_type=jnp.float32, precision=lax.Precision.HIGHEST
    )
    out_ref[...] = jnp.transpose(mixed)[:own, :].astype(jnp.bfloat16)

    @pl.when(core == 1)
    def _():
        back_zero.wait_send()

    back_one.wait_send()
    pltpu.make_async_copy(back_out.at[:, most], back_out.at[:, most], back_sem.at[0]).wait()


def shards(tokens, norm_gain, router, routes, w_gate_up, w_down):
    tok, width = tokens.shape
    columns = width // CHIPS
    half = NZ * CAP
    units = w_down.shape[1]
    experts = router.shape[1]
    group = tok // PIPE
    bf16, f32 = jnp.bfloat16, jnp.float32
    dma = pltpu.SemaphoreType.DMA
    anywhere = pl.BlockSpec(memory_space=pl.ANY)
    vmem = pl.BlockSpec(memory_space=pltpu.VMEM)
    mixed = pl.pallas_call(
        kernel,
        out_shape=jax.ShapeDtypeStruct((width // PIPE, tok), bf16),
        in_specs=[anywhere, vmem, anywhere, vmem, anywhere, anywhere],
        out_specs=vmem,
        scratch_shapes=[
            pltpu.VMEM((tok, width), bf16),
            pltpu.VMEM((columns, experts), bf16),
            pltpu.VMEM((width, CORES * 2 * units), bf16),
            pltpu.VMEM((CHIPS, CORES, units, columns), bf16),
            pltpu.VMEM((2, NZ, PIECE, LANES), bf16),
            pltpu.VMEM((2, NZ, PIECE, LANES), bf16),
            pltpu.VMEM((CHIPS, half, PARTS[0][1] * LANES), bf16),
            pltpu.VMEM((CHIPS, half, PARTS[1][1] * LANES), bf16),
            pltpu.VMEM((CHIPS, half, CORES * units), bf16),
            pltpu.VMEM((CORES, NZ, 32, LANES), bf16),
            pltpu.VMEM((HALVES, NZ, 32, LANES), bf16),
            pltpu.VMEM((PIPE, group, experts), f32),
            pltpu.VMEM((PIPE, group, experts), f32),
            pltpu.VMEM((group, 2 * half), f32),
            pltpu.VMEM((PIPE, group, 2 * half), f32),
            dma((7,)), dma((4,)), dma((4,)),
            dma((32,)), dma((4 * CHIPS,)), dma((4,)),
            dma((2 * CHIPS,)), dma((CHIPS,)), dma((CHIPS,)),
            dma((2,)), dma((4,)), dma((2,)), dma((2,)),
        ],
        compiler_params=pltpu.CompilerParams(
            collective_id=0, has_side_effects=True, vmem_limit_bytes=56 * 1024 * 1024
        ),
        cost_estimate=pl.CostEstimate(
            flops=2_000_000_000, bytes_accessed=8_000_000, transcendentals=100_000
        ),
    )(tokens, norm_gain.reshape(1, width), router, routes.T, w_gate_up, w_down)
    return mixed.T


def solution(mesh):
    placed = (
        P("ep", None),
        P(),
        P("pipe", None),
        P("ep", None),
        P("ep", None, "pipe"),
        P("ep", "pipe", None),
    )
    return jax.shard_map(
        shards, mesh=mesh, in_specs=placed, out_specs=P("ep", "pipe"), check_vma=False
    )
```

```python
import functools

import jax
import jax.numpy as jnp
from jax import lax
from jax.experimental import pallas as pl
from jax.experimental.pallas import tpu as pltpu
from jax.sharding import PartitionSpec as P

CORES = 2
NX = 4
NY = 2
CHIPS = NX * NY
PIPE = CHIPS * CORES
NZ = 16
HALVES = 2
CAP = 8
PARTS = ((0, 4), (4, 3))
PIECE = 32
LANES = 128
MESH = pl.DeviceIdType.MESH


def remote(src, dst, send, recv, pipe, ep):
    return pltpu.make_async_remote_copy(
        src_ref=src,
        dst_ref=dst,
        send_sem=send,
        recv_sem=recv,
        device_id=(pipe, ep),
        device_id_type=MESH,
    )


def one_hot(names, first, count, width):
    row = lax.broadcasted_iota(jnp.int32, (width, names.shape[1]), 0)
    expert = first + row // count
    named = names[0:1, :] == expert
    for k in range(1, names.shape[0]):
        named = named | (names[k : k + 1, :] == expert)
    return jnp.where(named, 1.0, 0.0), row


def slot_matrix(names, first, width):
    named, row = one_hot(names, first, CAP, width)
    tok = names.shape[1]
    earlier = lax.broadcasted_iota(jnp.int32, (tok, tok), 0) < lax.broadcasted_iota(
        jnp.int32, (tok, tok), 1
    )
    rank = jnp.dot(
        named.astype(jnp.bfloat16),
        jnp.where(earlier, 1.0, 0.0).astype(jnp.bfloat16),
        preferred_element_type=jnp.float32,
    )
    return jnp.where(rank == (row % CAP).astype(jnp.float32), named, 0.0)


def kernel(
    tokens_hbm, gain_ref, router_hbm, routes_ref, gate_up_hbm, down_hbm, out_ref,
    tokens, router, gate_up, down_a, down_b,
    outbox, inbox, rows_a, rows_b, hidden, back_out, back_in,
    score_out, score_in, weight_out, weight_in,
    load_sem, near_sem, out_sem, gather_send, gather_recv, pair_sem,
    down_sem, hidden_send, hidden_recv, back_sem, back_near,
    score_sem, weight_sem,
):
    pipe, ep = lax.axis_index("pipe"), lax.axis_index("ep")
    core, chip = lax.rem(pipe, CORES), lax.div(pipe, CORES)
    x, y = lax.rem(chip, NX), lax.div(chip, NX)
    z, side = lax.rem(ep, NZ), lax.div(ep, NZ)
    far_side = lax.rem(side + core, HALVES)
    partner = pipe + 1 - 2 * core
    tok, width = tokens.shape
    columns = width // CHIPS
    tiles = columns // LANES
    half = NZ * CAP
    own = columns // CORES
    units = down_a.shape[2]
    downs = (down_a, down_b)
    total_slots = HALVES * half

    def column_block(which):
        return pl.ds(pl.multiple_of(which * columns, LANES), columns)

    def down_columns(part, which):
        first, count = PARTS[part]
        start = pl.multiple_of(which * columns + first * LANES, LANES)
        return down_hbm.at[0, :, pl.ds(start, count * LANES)]

    def far_first(i):
        return lax.rem(z + NZ // 2 + lax.div(i, 2) * (1 - 2 * lax.rem(i, 2)), NZ)

    own_lanes = pl.ds(pl.multiple_of(core * 2 * units, LANES), 2 * units)
    quarter = width // 4
    token_loads = [
        pltpu.make_async_copy(
            tokens_hbm.at[:, pl.ds(n * quarter, quarter)],
            tokens.at[:, pl.ds(n * quarter, quarter)],
            load_sem.at[4 + n],
        )
        for n in range(4)
    ]
    for load in token_loads:
        load.start()

    barrier = pltpu.get_barrier_semaphore()

    def greet_pipe(i, _):
        pl.semaphore_signal(
            barrier, inc=1, device_id=(lax.rem(pipe + i, PIPE), ep), device_id_type=MESH
        )
        return 0

    lax.fori_loop(1, PIPE, greet_pipe, 0)

    def greet_ep(i, _):
        other = lax.rem(z + i, NZ)
        for k in range(CORES):
            pl.semaphore_signal(
                barrier, inc=1,
                device_id=(CORES * chip + k, lax.rem(side + k, HALVES) * NZ + other),
                device_id_type=MESH,
            )
        return 0

    lax.fori_loop(1, NZ, greet_ep, 0)
    pl.semaphore_signal(
        barrier, inc=1,
        device_id=(CORES * chip + 1, (1 - side) * NZ + z), device_id_type=MESH,
    )

    @pl.when(core == 1)
    def _():
        pl.semaphore_signal(barrier, inc=1, device_id=(partner, ep), device_id_type=MESH)

    names = routes_ref[...]
    placing = slot_matrix(names, lax.rem(core + side, HALVES) * NZ, half).astype(jnp.bfloat16)

    squares = jnp.zeros((tok, LANES), jnp.float32)
    for n in range(4):
        token_loads[n].wait()
        for at in range(n * quarter // LANES, (n + 1) * quarter // LANES):
            values = tokens[:, at * LANES : (at + 1) * LANES].astype(jnp.float32)
            squares += values * values
    router[...] = jnp.zeros_like(router)
    loads = [
        pltpu.make_async_copy(src, dst, load_sem.at[number])
        for number, (src, dst) in enumerate(
            ((router_hbm, router.at[pl.ds(core * own, own), :]),
             (gate_up_hbm.at[0], gate_up.at[:, own_lanes]),
             (down_columns(0, chip), down_a.at[chip, core]),
             (down_columns(1, chip), down_b.at[chip, core]))
        )
    ]
    for load in loads:
        load.start()
    scale = lax.rsqrt(jnp.sum(squares, axis=1, keepdims=True) / width + 1e-06)
    block = column_block(chip)
    normed = (tokens[:, block].astype(jnp.float32) * scale * gain_ref[:, block]).astype(
        jnp.bfloat16
    )
    placed = jnp.dot(placing, normed, preferred_element_type=jnp.float32)
    for part, (first, count) in enumerate(PARTS):
        pieces = [
            placed[:, at * LANES : (at + 1) * LANES].reshape(NZ, CAP, LANES)
            for at in range(first, first + count)
        ]
        if count < 4:
            pieces.append(jnp.zeros((NZ, PIECE - count * CAP, LANES), jnp.float32))
        outbox[part] = jnp.concatenate(pieces, axis=1).astype(jnp.bfloat16)

    pl.semaphore_wait(barrier, PIPE - 1 + 2 * NZ - 1 + core)

    def near_copy(part):
        return remote(
            outbox.at[part, z], inbox.at[part, z],
            near_sem.at[2 * part], near_sem.at[2 * part + 1], pipe, far_side * NZ + z,
        )

    def send_rows(part):
        def dispatch(i, _):
            other = far_first(i)
            remote(
                outbox.at[part, other], inbox.at[part, z],
                out_sem.at[2 * part], out_sem.at[2 * part + 1],
                pipe, far_side * NZ + other,
            ).start()
            return 0

        lax.fori_loop(1, NZ, dispatch, 0)

        @pl.when(core == 1)
        def _():
            near_copy(part).start()

        @pl.when(core == 0)
        def _():
            pltpu.make_async_copy(
                outbox.at[part, z], inbox.at[part, z], near_sem.at[2 * part + 1]
            ).start()

    def rows_left(part):
        pltpu.make_async_copy(
            outbox.at[part, most], outbox.at[part, most], out_sem.at[2 * part]
        ).wait()

        @pl.when(core == 1)
        def _():
            near_copy(part).wait_send()

    most = pl.ds(0, NZ - 1)
    send_rows(0)

    def chip_at(ry, rx):
        return lax.rem(y + ry, NY) * NX + lax.rem(x + rx, NX)

    relative = [(ry, rx) for rx in (2, 1, 3, 0) for ry in (1, 0) if (ry, rx) != (0, 0)]
    mirror = {(ry, rx): ry * NX + (NX - rx) % NX for ry, rx in relative}

    def down_to(part, ry, rx):
        return remote(
            down_columns(part, chip_at(ry, rx)), downs[part].at[chip, core],
            down_sem.at[part, ry * NX + rx], down_sem.at[part, CHIPS + mirror[ry, rx]],
            CORES * chip_at(ry, rx) + core, ep,
        )

    def down_pair(part):
        return remote(
            downs[part].at[:, core], downs[part].at[:, core],
            pair_sem.at[2 + 2 * part], pair_sem.at[3 + 2 * part], partner, ep,
        )

    def share_down(part):
        loads[2 + part].wait()
        for ry, rx in relative:
            down_to(part, ry, rx).wait_recv()
        down_pair(part).start()

    for ry, rx in relative:
        down_to(0, ry, rx).start()
    gate_up_pair = remote(
        gate_up_hbm.at[0], gate_up.at[:, own_lanes], pair_sem.at[0], pair_sem.at[1], partner, ep
    )
    gate_up_pair.start()

    loads[0].wait()
    scores = jnp.dot(normed, router[...], preferred_element_type=jnp.float32)
    score_out[...] = scores.reshape(score_out.shape)
    score_in[pipe] = score_out[pipe]

    def send_scores(i, _):
        other = lax.rem(pipe + i, PIPE)
        remote(
            score_out.at[other], score_in.at[pipe], score_sem.at[0], score_sem.at[1], other, ep
        ).start()
        return 0

    lax.fori_loop(1, PIPE, send_scores, 0)

    rows_left(0)
    send_rows(1)

    gathered = (rows_a, rows_b)
    sent = []

    def arrive(part):
        first, count = PARTS[part]
        pltpu.make_async_copy(
            inbox.at[part, most], inbox.at[part, most], out_sem.at[2 * part + 1]
        ).wait()
        pltpu.make_async_copy(
            inbox.at[part, 0], inbox.at[part, 0], near_sem.at[2 * part + 1]
        ).wait()
        arrived = inbox[part].astype(jnp.float32)
        for at in range(count):
            gathered[part][chip, :, at * LANES : (at + 1) * LANES] = (
                arrived[:, at * CAP : (at + 1) * CAP, :].reshape(half, LANES).astype(jnp.bfloat16)
            )

    def block_ref(part, ry, rx, piece):
        ref = gathered[part].at[chip_at(ry, rx)]
        return ref if piece is None else ref.at[pl.ds(piece * (half // 2), half // 2), :]

    def recv_sem(part, ry, rx, piece):
        return gather_recv.at[(part * CHIPS + (ry % NY) * NX + rx % NX) * 2 + (piece or 0)]

    def pass_on(part, block, target, piece=None):
        (ry, rx), (ty, tx) = block, target
        ref = block_ref(part, ry, rx, piece)
        copy = remote(
            ref, ref, gather_send.at[len(sent)], recv_sem(part, ry + ty, rx - tx + NX, piece),
            CORES * chip_at(ty, tx) + core, ep,
        )
        copy.start()
        sent.append(copy)

    def take(part, ry, rx, piece=None):
        ref = block_ref(part, ry, rx, piece)
        pltpu.make_async_copy(ref, ref, recv_sem(part, ry, rx, piece)).wait()

    up, plus, minus = (1, 0), (0, 1), (0, 3)

    arrive(0)
    for target in (plus, minus, up):
        pass_on(0, (0, 0), target)

    take(0, 1, 0)
    pass_on(0, (1, 0), plus)
    pass_on(0, (1, 0), minus)
    for ry in range(NY):
        take(0, ry, 3)
        pass_on(0, (ry, 3), plus, 0)
        take(0, ry, 1)
        pass_on(0, (ry, 1), minus, 1)

    arrive(1)
    for target in (plus, minus, up):
        pass_on(1, (0, 0), target)

    share_down(0)

    most_pipe = pl.ds(0, PIPE - 1)
    pltpu.make_async_copy(score_in.at[most_pipe], score_in.at[most_pipe], score_sem.at[1]).wait()
    affinity = jax.nn.sigmoid(jnp.sum(score_in[...], axis=0))
    group, experts = affinity.shape
    pick_token = lax.broadcasted_iota(jnp.int32, (group, tok), 1)
    pick_row = lax.broadcasted_iota(jnp.int32, (group, tok), 0)
    pick = jnp.where(pick_token == pick_row + pipe * group, 1.0, 0.0).astype(jnp.bfloat16)
    chosen_all, _ = one_hot(names, 0, 1, experts)
    chosen = lax.dot_general(
        pick, chosen_all.astype(jnp.bfloat16), (((1,), (1,)), ((), ())),
        preferred_element_type=jnp.float32,
    )
    fraction = 2.5 * affinity / jnp.sum(chosen * affinity, axis=1, keepdims=True)
    spread_row = lax.broadcasted_iota(jnp.int32, (experts, total_slots), 0)
    spread_lane = lax.broadcasted_iota(jnp.int32, (experts, total_slots), 1)
    slot_expert = lax.rem(spread_lane // CAP + side * NZ, HALVES * NZ)
    weight_out[...] = jnp.dot(
        fraction, jnp.where(spread_row == slot_expert, 1.0, 0.0),
        preferred_element_type=jnp.float32, precision=lax.Precision.HIGHEST,
    )
    weight_in[pipe] = weight_out[...]

    def send_weights(i, _):
        other = lax.rem(pipe + i, PIPE)
        remote(weight_out, weight_in.at[pipe], weight_sem.at[0], weight_sem.at[1], other, ep).start()
        return 0

    lax.fori_loop(1, PIPE, send_weights, 0)

    loads[1].wait()
    gate_up_pair.wait_recv()

    def project(part, ry, rx):
        first, count = PARTS[part]
        which = chip_at(ry, rx)
        start = pl.multiple_of(which * columns + first * LANES, LANES)
        return jnp.dot(
            gathered[part][which], gate_up[pl.ds(start, count * LANES), :],
            preferred_element_type=jnp.float32,
        )

    both = project(0, 0, 0) + project(0, 1, 0)
    take(1, 0, 3)
    pass_on(1, (0, 3), plus, 0)
    pass_on(1, (0, 3), up)
    take(1, 0, 1)
    pass_on(1, (0, 1), minus, 1)
    pass_on(1, (0, 1), up)
    for ry in range(NY):
        both += project(0, ry, 3) + project(0, ry, 1)
    for piece in range(2):
        take(1, 0, 2, piece)
        pass_on(1, (0, 2), up, piece)
    for ry, rx in relative:
        down_to(1, ry, rx).start()
    both += project(1, 0, 0) + project(1, 0, 1) + project(1, 0, 2) + project(1, 0, 3)
    for ry in range(NY):
        for piece in range(2):
            take(0, ry, 2, piece)
        both += project(0, ry, 2)
    for rx in (0, 3, 1):
        take(1, 1, rx)
        both += project(1, 1, rx)
    for piece in range(2):
        take(1, 1, 2, piece)
    both += project(1, 1, 2)
    parts = []
    for k in range(CORES):
        gate = both[:, 2 * k * units : (2 * k + 1) * units]
        upper = both[:, (2 * k + 1) * units : (2 * k + 2) * units]
        parts.append(gate / (1.0 + jnp.exp(-gate)) * upper)
    hidden[chip] = jnp.concatenate(parts, axis=1).astype(jnp.bfloat16)

    def hidden_to(ry, rx):
        return remote(
            hidden.at[chip], hidden.at[chip],
            hidden_send.at[ry * NX + rx], hidden_recv.at[mirror[ry, rx]],
            CORES * chip_at(ry, rx) + core, ep,
        )

    for ry, rx in relative:
        hidden_to(ry, rx).start()

    down_pair(0).wait_recv()
    order = [(1, 0), (0, 1), (0, 3), (1, 1), (1, 3), (0, 2), (1, 2)]

    def lower(part, ry, rx):
        which = chip_at(ry, rx)
        return jnp.dot(
            hidden[which], downs[part][which].reshape(CORES * units, PARTS[part][1] * LANES),
            preferred_element_type=jnp.float32,
        )

    def go_back(j, result):
        pieces = []
        for at in range(4):
            low, high = at * LANES, min((at + 1) * LANES, own)
            piece = result[:, low:high]
            if high - low < LANES:
                piece = jnp.concatenate(
                    [piece, jnp.zeros((half, LANES - (high - low)), jnp.float32)], axis=1
                )
            pieces.append(piece.reshape(NZ, CAP, LANES))
        back_out[j] = jnp.concatenate(pieces, axis=1).astype(jnp.bfloat16)

        def go(i, _):
            other = far_first(i)
            remote(
                back_out.at[j, other], back_in.at[core, z], back_sem.at[0], back_sem.at[1],
                CORES * chip + j, far_side * NZ + other,
            ).start()
            return 0

        lax.fori_loop(1, NZ, go, 0)

    low_part = lower(0, 0, 0)
    for ry, rx in order:
        hidden_to(ry, (NX - rx) % NX).wait_recv()
        low_part += lower(0, ry, rx)
    go_back(0, low_part)
    back_zero = remote(
        back_out.at[0, z], back_in.at[core, z], back_near.at[0], back_near.at[2 + core],
        CORES * chip, far_side * NZ + z,
    )

    @pl.when(core == 1)
    def _():
        back_zero.start()

    @pl.when(core == 0)
    def _():
        pltpu.make_async_copy(
            back_out.at[0, z], back_in.at[core, z], back_near.at[2 + core]
        ).start()

    share_down(1)
    down_pair(1).wait_recv()
    high_part = lower(1, 0, 0)
    for ry, rx in order:
        high_part += lower(1, ry, rx)
    go_back(1, jnp.concatenate([low_part[:, own:], high_part], axis=1))
    back_one = remote(
        back_out.at[1, z], back_in.at[core, z], back_near.at[1], back_near.at[2 + core],
        CORES * chip + 1, far_side * NZ + z,
    )
    back_one.start()

    slots_all = slot_matrix(names, 0, total_slots)
    slots_now = jnp.where(
        side == 0, slots_all, jnp.concatenate([slots_all[half:], slots_all[:half]], axis=0)
    )
    pltpu.make_async_copy(
        weight_in.at[most_pipe], weight_in.at[most_pipe], weight_sem.at[1]
    ).wait()
    combining = jnp.transpose(slots_now) * weight_in[...].reshape(tok, total_slots)
    chip_tokens = tokens[:, block].astype(jnp.float32)
    padding = jnp.zeros((tok, 4 * LANES - own), jnp.float32)
    residual = jnp.where(
        core == 0, chip_tokens[:, : 4 * LANES],
        jnp.concatenate([chip_tokens[:, own:], padding], axis=1),
    )

    rows_left(1)
    pltpu.make_async_copy(
        score_out.at[most_pipe], score_out.at[most_pipe], score_sem.at[0]
    ).wait()
    pltpu.make_async_copy(
        weight_in.at[most_pipe], weight_in.at[most_pipe], weight_sem.at[0]
    ).wait()
    for ry, rx in relative:
        down_to(0, ry, rx).wait_send()
        down_to(1, ry, rx).wait_send()
        hidden_to(ry, rx).wait_send()
    for copy in sent:
        copy.wait_send()
    gate_up_pair.wait_send()
    down_pair(0).wait_send()
    down_pair(1).wait_send()

    pltpu.make_async_copy(
        back_in.at[:, most], back_in.at[:, most], back_sem.at[1]
    ).wait()
    for k in range(HALVES):
        pltpu.make_async_copy(back_in.at[k, 0], back_in.at[k, 0], back_near.at[2 + k]).wait()
    returned = back_in[...].astype(jnp.float32)
    returned = jnp.concatenate(
        [
            returned[:, :, at * CAP : (at + 1) * CAP, :].reshape(total_slots, LANES)
            for at in range(4)
        ],
        axis=1,
    )
    mixed = residual + jnp.dot(
        combining, returned, preferred_element_type=jnp.float32, precision=lax.Precision.HIGHEST
    )
    out_ref[...] = jnp.transpose(mixed)[:own, :].astype(jnp.bfloat16)

    @pl.when(core == 1)
    def _():
        back_zero.wait_send()

    back_one.wait_send()
    pltpu.make_async_copy(back_out.at[:, most], back_out.at[:, most], back_sem.at[0]).wait()


def shards(tokens, norm_gain, router, routes, w_gate_up, w_down):
    tok, width = tokens.shape
    columns = width // CHIPS
    half = NZ * CAP
    units = w_down.shape[1]
    experts = router.shape[1]
    group = tok // PIPE
    bf16, f32 = jnp.bfloat16, jnp.float32
    dma = pltpu.SemaphoreType.DMA
    anywhere = pl.BlockSpec(memory_space=pl.ANY)
    vmem = pl.BlockSpec(memory_space=pltpu.VMEM)
    mixed = pl.pallas_call(
        kernel,
        out_shape=jax.ShapeDtypeStruct((width // PIPE, tok), bf16),
        in_specs=[anywhere, vmem, anywhere, vmem, anywhere, anywhere],
        out_specs=vmem,
        scratch_shapes=[
            pltpu.VMEM((tok, width), bf16),
            pltpu.VMEM((columns, experts), bf16),
            pltpu.VMEM((width, CORES * 2 * units), bf16),
            pltpu.VMEM((CHIPS, CORES, units, PARTS[0][1] * LANES), bf16),
            pltpu.VMEM((CHIPS, CORES, units, PARTS[1][1] * LANES), bf16),
            pltpu.VMEM((2, NZ, PIECE, LANES), bf16),
            pltpu.VMEM((2, NZ, PIECE, LANES), bf16),
            pltpu.VMEM((CHIPS, half, PARTS[0][1] * LANES), bf16),
            pltpu.VMEM((CHIPS, half, PARTS[1][1] * LANES), bf16),
            pltpu.VMEM((CHIPS, half, CORES * units), bf16),
            pltpu.VMEM((CORES, NZ, 32, LANES), bf16),
            pltpu.VMEM((HALVES, NZ, 32, LANES), bf16),
            pltpu.VMEM((PIPE, group, experts), f32),
            pltpu.VMEM((PIPE, group, experts), f32),
            pltpu.VMEM((group, 2 * half), f32),
            pltpu.VMEM((PIPE, group, 2 * half), f32),
            dma((8,)), dma((4,)), dma((4,)),
            dma((32,)), dma((4 * CHIPS,)), dma((6,)),
            dma((2, 2 * CHIPS)), dma((CHIPS,)), dma((CHIPS,)),
            dma((2,)), dma((4,)), dma((2,)), dma((2,)),
        ],
        compiler_params=pltpu.CompilerParams(
            collective_id=0, has_side_effects=True, vmem_limit_bytes=56 * 1024 * 1024
        ),
        cost_estimate=pl.CostEstimate(
            flops=2_000_000_000, bytes_accessed=8_000_000, transcendentals=100_000
        ),
    )(tokens, norm_gain.reshape(1, width), router, routes.T, w_gate_up, w_down)
    return mixed.T


def solution(mesh):
    placed = (
        P("ep", None),
        P(),
        P("pipe", None),
        P("ep", None),
        P("ep", None, "pipe"),
        P("ep", "pipe", None),
    )
    return jax.shard_map(
        shards, mesh=mesh, in_specs=placed, out_specs=P("ep", "pipe"), check_vma=False
    )
```

```python
import functools

import jax
import jax.numpy as jnp
from jax import lax
from jax.experimental import pallas as pl
from jax.experimental.pallas import tpu as pltpu
from jax.sharding import PartitionSpec as P

CORES = 2
NX = 4
NY = 2
CHIPS = NX * NY
PIPE = CHIPS * CORES
NZ = 16
HALVES = 2
CAP = 8
PARTS = ((0, 2), (2, 2), (4, 2), (6, 1))
DOWN_PARTS = ((0, 4), (4, 3))
PIECE = 16
Y_FIRST = (0, 2)
ARRIVALS = (
    (0, 0, 0, None), (1, 0, 0, None), (0, 1, 0, None), (0, 0, 3, None), (0, 0, 1, None),
    (2, 0, 0, None), (1, 0, 3, None), (1, 0, 1, None), (1, 1, 0, None), (0, 1, 3, None),
    (0, 1, 1, None), (3, 0, 0, None), (0, 0, 2, 0), (0, 0, 2, 1), (2, 1, 0, None),
    (2, 0, 3, None), (2, 0, 1, None), (1, 1, 3, None), (1, 0, 2, 0), (1, 0, 2, 1),
    (0, 1, 2, 0), (0, 1, 2, 1), (1, 1, 1, None), (3, 0, 3, None), (3, 0, 1, None),
    (3, 1, 0, None), (2, 1, 3, None), (2, 1, 1, None), (1, 1, 2, 0), (1, 1, 2, 1),
    (2, 0, 2, 0), (2, 0, 2, 1), (3, 0, 2, 0), (3, 0, 2, 1), (3, 1, 3, None),
    (3, 1, 1, None), (2, 1, 2, 0), (2, 1, 2, 1), (3, 1, 2, 0), (3, 1, 2, 1),
)
LANES = 128
MESH = pl.DeviceIdType.MESH


def remote(src, dst, send, recv, pipe, ep):
    return pltpu.make_async_remote_copy(
        src_ref=src,
        dst_ref=dst,
        send_sem=send,
        recv_sem=recv,
        device_id=(pipe, ep),
        device_id_type=MESH,
    )


def one_hot(names, first, count, width):
    row = lax.broadcasted_iota(jnp.int32, (width, names.shape[1]), 0)
    expert = first + row // count
    named = names[0:1, :] == expert
    for k in range(1, names.shape[0]):
        named = named | (names[k : k + 1, :] == expert)
    return jnp.where(named, 1.0, 0.0), row


def slot_matrix(names, first, width):
    named, row = one_hot(names, first, CAP, width)
    tok = names.shape[1]
    earlier = lax.broadcasted_iota(jnp.int32, (tok, tok), 0) < lax.broadcasted_iota(
        jnp.int32, (tok, tok), 1
    )
    rank = jnp.dot(
        named.astype(jnp.bfloat16),
        jnp.where(earlier, 1.0, 0.0).astype(jnp.bfloat16),
        preferred_element_type=jnp.float32,
    )
    return jnp.where(rank == (row % CAP).astype(jnp.float32), named, 0.0)


def kernel(
    tokens_hbm, gain_ref, router_hbm, routes_ref, gate_up_hbm, down_hbm, out_ref,
    tokens, router, gate_up, down_a, down_b,
    outbox, inbox, rows_a, rows_b, rows_c, rows_d, hidden, back_out, back_in,
    score_out, score_in, weight_out, weight_in,
    load_sem, near_sem, out_sem, gather_send, gather_recv, pair_sem,
    down_sem, hidden_send, hidden_recv, back_sem, back_near,
    score_sem, weight_sem,
):
    pipe, ep = lax.axis_index("pipe"), lax.axis_index("ep")
    core, chip = lax.rem(pipe, CORES), lax.div(pipe, CORES)
    x, y = lax.rem(chip, NX), lax.div(chip, NX)
    z, side = lax.rem(ep, NZ), lax.div(ep, NZ)
    far_side = lax.rem(side + core, HALVES)
    partner = pipe + 1 - 2 * core
    tok, width = tokens.shape
    columns = width // CHIPS
    tiles = columns // LANES
    half = NZ * CAP
    own = columns // CORES
    units = down_a.shape[2]
    downs = (down_a, down_b)
    total_slots = HALVES * half

    def column_block(which):
        return pl.ds(pl.multiple_of(which * columns, LANES), columns)

    def down_columns(part, which):
        first, count = DOWN_PARTS[part]
        start = pl.multiple_of(which * columns + first * LANES, LANES)
        return down_hbm.at[0, :, pl.ds(start, count * LANES)]

    def far_first(i):
        return lax.rem(z + NZ // 2 + lax.div(i, 2) * (1 - 2 * lax.rem(i, 2)), NZ)

    own_lanes = pl.ds(pl.multiple_of(core * 2 * units, LANES), 2 * units)
    quarter = width // 4
    token_loads = [
        pltpu.make_async_copy(
            tokens_hbm.at[:, pl.ds(n * quarter, quarter)],
            tokens.at[:, pl.ds(n * quarter, quarter)],
            load_sem.at[4 + n],
        )
        for n in range(4)
    ]
    for load in token_loads:
        load.start()

    barrier = pltpu.get_barrier_semaphore()

    def greet_pipe(i, _):
        pl.semaphore_signal(
            barrier, inc=1, device_id=(lax.rem(pipe + i, PIPE), ep), device_id_type=MESH
        )
        return 0

    lax.fori_loop(1, PIPE, greet_pipe, 0)

    def greet_ep(i, _):
        other = lax.rem(z + i, NZ)
        for k in range(CORES):
            pl.semaphore_signal(
                barrier, inc=1,
                device_id=(CORES * chip + k, lax.rem(side + k, HALVES) * NZ + other),
                device_id_type=MESH,
            )
        return 0

    lax.fori_loop(1, NZ, greet_ep, 0)
    pl.semaphore_signal(
        barrier, inc=1,
        device_id=(CORES * chip + 1, (1 - side) * NZ + z), device_id_type=MESH,
    )

    @pl.when(core == 1)
    def _():
        pl.semaphore_signal(barrier, inc=1, device_id=(partner, ep), device_id_type=MESH)

    names = routes_ref[...]
    placing = slot_matrix(names, lax.rem(core + side, HALVES) * NZ, half).astype(jnp.bfloat16)

    squares = jnp.zeros((tok, LANES), jnp.float32)
    for n in range(4):
        token_loads[n].wait()
        for at in range(n * quarter // LANES, (n + 1) * quarter // LANES):
            values = tokens[:, at * LANES : (at + 1) * LANES].astype(jnp.float32)
            squares += values * values
    router[...] = jnp.zeros_like(router)
    loads = [
        pltpu.make_async_copy(src, dst, load_sem.at[number])
        for number, (src, dst) in enumerate(
            ((router_hbm, router.at[pl.ds(core * own, own), :]),
             (gate_up_hbm.at[0], gate_up.at[:, own_lanes]),
             (down_columns(0, chip), down_a.at[chip, core]),
             (down_columns(1, chip), down_b.at[chip, core]))
        )
    ]
    for load in loads:
        load.start()
    scale = lax.rsqrt(jnp.sum(squares, axis=1, keepdims=True) / width + 1e-06)
    block = column_block(chip)
    normed = (tokens[:, block].astype(jnp.float32) * scale * gain_ref[:, block]).astype(
        jnp.bfloat16
    )
    placed = jnp.dot(placing, normed, preferred_element_type=jnp.float32)
    for part, (first, count) in enumerate(PARTS):
        pieces = [
            placed[:, at * LANES : (at + 1) * LANES].reshape(NZ, CAP, LANES)
            for at in range(first, first + count)
        ]
        if count * CAP < PIECE:
            pieces.append(jnp.zeros((NZ, PIECE - count * CAP, LANES), jnp.float32))
        outbox[part] = jnp.concatenate(pieces, axis=1).astype(jnp.bfloat16)

    pl.semaphore_wait(barrier, PIPE - 1 + 2 * NZ - 1 + core)

    def near_copy(part):
        return remote(
            outbox.at[part, z], inbox.at[part, z],
            near_sem.at[2 * part], near_sem.at[2 * part + 1], pipe, far_side * NZ + z,
        )

    def send_rows(part):
        def dispatch(i, _):
            other = far_first(i)
            remote(
                outbox.at[part, other], inbox.at[part, z],
                out_sem.at[2 * part], out_sem.at[2 * part + 1],
                pipe, far_side * NZ + other,
            ).start()
            return 0

        lax.fori_loop(1, NZ, dispatch, 0)

        @pl.when(core == 1)
        def _():
            near_copy(part).start()

        @pl.when(core == 0)
        def _():
            pltpu.make_async_copy(
                outbox.at[part, z], inbox.at[part, z], near_sem.at[2 * part + 1]
            ).start()

    def rows_left(part):
        pltpu.make_async_copy(
            outbox.at[part, most], outbox.at[part, most], out_sem.at[2 * part]
        ).wait()

        @pl.when(core == 1)
        def _():
            near_copy(part).wait_send()

    most = pl.ds(0, NZ - 1)
    send_rows(0)

    def chip_at(ry, rx):
        return lax.rem(y + ry, NY) * NX + lax.rem(x + rx, NX)

    relative = [(ry, rx) for rx in (2, 1, 3, 0) for ry in (1, 0) if (ry, rx) != (0, 0)]
    mirror = {(ry, rx): ry * NX + (NX - rx) % NX for ry, rx in relative}

    def down_to(part, ry, rx):
        return remote(
            down_columns(part, chip_at(ry, rx)), downs[part].at[chip, core],
            down_sem.at[part, ry * NX + rx], down_sem.at[part, CHIPS + mirror[ry, rx]],
            CORES * chip_at(ry, rx) + core, ep,
        )

    def down_pair(part):
        return remote(
            downs[part].at[:, core], downs[part].at[:, core],
            pair_sem.at[2 + 2 * part], pair_sem.at[3 + 2 * part], partner, ep,
        )

    def share_down(part):
        loads[2 + part].wait()
        for ry, rx in relative:
            down_to(part, ry, rx).wait_recv()
        down_pair(part).start()

    for ry, rx in relative:
        down_to(0, ry, rx).start()
    gate_up_pair = remote(
        gate_up_hbm.at[0], gate_up.at[:, own_lanes], pair_sem.at[0], pair_sem.at[1], partner, ep
    )
    gate_up_pair.start()

    loads[0].wait()
    scores = jnp.dot(normed, router[...], preferred_element_type=jnp.float32)
    score_out[...] = scores.reshape(score_out.shape)
    score_in[pipe] = score_out[pipe]

    def send_scores(i, _):
        other = lax.rem(pipe + i, PIPE)
        remote(
            score_out.at[other], score_in.at[pipe], score_sem.at[0], score_sem.at[1], other, ep
        ).start()
        return 0

    lax.fori_loop(1, PIPE, send_scores, 0)

    for part in range(1, len(PARTS) - 1):
        rows_left(part - 1)
        send_rows(part)

    gathered = (rows_a, rows_b, rows_c, rows_d)
    sent = []

    def arrive(part):
        first, count = PARTS[part]
        pltpu.make_async_copy(
            inbox.at[part, most], inbox.at[part, most], out_sem.at[2 * part + 1]
        ).wait()
        pltpu.make_async_copy(
            inbox.at[part, 0], inbox.at[part, 0], near_sem.at[2 * part + 1]
        ).wait()
        arrived = inbox[part].astype(jnp.float32)
        for at in range(count):
            gathered[part][chip, :, at * LANES : (at + 1) * LANES] = (
                arrived[:, at * CAP : (at + 1) * CAP, :].reshape(half, LANES).astype(jnp.bfloat16)
            )

    def block_ref(part, ry, rx, piece):
        ref = gathered[part].at[chip_at(ry, rx)]
        return ref if piece is None else ref.at[pl.ds(piece * (half // 2), half // 2), :]

    def recv_sem(part, ry, rx, piece):
        return gather_recv.at[(part * CHIPS + (ry % NY) * NX + rx % NX) * 2 + (piece or 0)]

    def pass_on(part, block, target, piece=None):
        (ry, rx), (ty, tx) = block, target
        ref = block_ref(part, ry, rx, piece)
        copy = remote(
            ref, ref, gather_send.at[len(sent)], recv_sem(part, ry + ty, rx - tx + NX, piece),
            CORES * chip_at(ty, tx) + core, ep,
        )
        copy.start()
        sent.append(copy)

    def take(part, ry, rx, piece=None):
        ref = block_ref(part, ry, rx, piece)
        pltpu.make_async_copy(ref, ref, recv_sem(part, ry, rx, piece)).wait()

    up, plus, minus = (1, 0), (0, 1), (0, 3)

    def project(part, ry, rx):
        first, count = PARTS[part]
        which = chip_at(ry, rx)
        start = pl.multiple_of(which * columns + first * LANES, LANES)
        return jnp.dot(
            gathered[part][which], gate_up[pl.ds(start, count * LANES), :],
            preferred_element_type=jnp.float32,
        )

    both = jnp.zeros((half, CORES * 2 * units), jnp.float32)
    for step, (part, ry, rx, piece) in enumerate(ARRIVALS):
        here = (ry, rx)
        if here == (0, 0):
            arrive(part)
            for target in (up, plus, minus) if part in Y_FIRST else (plus, minus, up):
                pass_on(part, here, target)
        else:
            take(part, ry, rx, piece)
            if part in Y_FIRST:
                if here == up:
                    pass_on(part, here, plus)
                    pass_on(part, here, minus)
            elif ry == 0 and rx == 2:
                pass_on(part, here, up, piece)
            if part in Y_FIRST or ry == 0:
                if rx == 3:
                    pass_on(part, here, plus, 0)
                elif rx == 1:
                    pass_on(part, here, minus, 1)
            if part not in Y_FIRST and ry == 0 and rx != 2:
                pass_on(part, here, up)
        if step == 0:
            rows_left(len(PARTS) - 2)
            send_rows(len(PARTS) - 1)
            loads[1].wait()
            gate_up_pair.wait_recv()
        if (part, ry, rx) == (len(PARTS) - 1, 0, 0):
            share_down(0)
        if piece != 0:
            both += project(part, ry, rx)
    parts = []
    for k in range(CORES):
        gate = both[:, 2 * k * units : (2 * k + 1) * units]
        upper = both[:, (2 * k + 1) * units : (2 * k + 2) * units]
        parts.append(gate / (1.0 + jnp.exp(-gate)) * upper)
    hidden[chip] = jnp.concatenate(parts, axis=1).astype(jnp.bfloat16)

    def hidden_to(ry, rx):
        return remote(
            hidden.at[chip], hidden.at[chip],
            hidden_send.at[ry * NX + rx], hidden_recv.at[mirror[ry, rx]],
            CORES * chip_at(ry, rx) + core, ep,
        )

    for ry, rx in relative:
        hidden_to(ry, rx).start()
    for ry, rx in relative:
        down_to(1, ry, rx).start()

    most_pipe = pl.ds(0, PIPE - 1)
    pltpu.make_async_copy(score_in.at[most_pipe], score_in.at[most_pipe], score_sem.at[1]).wait()
    affinity = jax.nn.sigmoid(jnp.sum(score_in[...], axis=0))
    group, experts = affinity.shape
    pick_token = lax.broadcasted_iota(jnp.int32, (group, tok), 1)
    pick_row = lax.broadcasted_iota(jnp.int32, (group, tok), 0)
    pick = jnp.where(pick_token == pick_row + pipe * group, 1.0, 0.0).astype(jnp.bfloat16)
    chosen_all, _ = one_hot(names, 0, 1, experts)
    chosen = lax.dot_general(
        pick, chosen_all.astype(jnp.bfloat16), (((1,), (1,)), ((), ())),
        preferred_element_type=jnp.float32,
    )
    fraction = 2.5 * affinity / jnp.sum(chosen * affinity, axis=1, keepdims=True)
    spread_row = lax.broadcasted_iota(jnp.int32, (experts, total_slots), 0)
    spread_lane = lax.broadcasted_iota(jnp.int32, (experts, total_slots), 1)
    slot_expert = lax.rem(spread_lane // CAP + side * NZ, HALVES * NZ)
    weight_out[...] = jnp.dot(
        fraction, jnp.where(spread_row == slot_expert, 1.0, 0.0),
        preferred_element_type=jnp.float32, precision=lax.Precision.HIGHEST,
    )
    weight_in[pipe] = weight_out[...]

    def send_weights(i, _):
        other = lax.rem(pipe + i, PIPE)
        remote(weight_out, weight_in.at[pipe], weight_sem.at[0], weight_sem.at[1], other, ep).start()
        return 0

    lax.fori_loop(1, PIPE, send_weights, 0)

    down_pair(0).wait_recv()
    order = [(1, 0), (0, 1), (0, 3), (1, 1), (1, 3), (0, 2), (1, 2)]

    def lower(part, ry, rx):
        which = chip_at(ry, rx)
        return jnp.dot(
            hidden[which], downs[part][which].reshape(CORES * units, DOWN_PARTS[part][1] * LANES),
            preferred_element_type=jnp.float32,
        )

    def go_back(j, result):
        pieces = []
        for at in range(4):
            low, high = at * LANES, min((at + 1) * LANES, own)
            piece = result[:, low:high]
            if high - low < LANES:
                piece = jnp.concatenate(
                    [piece, jnp.zeros((half, LANES - (high - low)), jnp.float32)], axis=1
                )
            pieces.append(piece.reshape(NZ, CAP, LANES))
        back_out[j] = jnp.concatenate(pieces, axis=1).astype(jnp.bfloat16)

        def go(i, _):
            other = far_first(i)
            remote(
                back_out.at[j, other], back_in.at[core, z], back_sem.at[0], back_sem.at[1],
                CORES * chip + j, far_side * NZ + other,
            ).start()
            return 0

        lax.fori_loop(1, NZ, go, 0)

    low_part = lower(0, 0, 0)
    for ry, rx in order:
        hidden_to(ry, (NX - rx) % NX).wait_recv()
        low_part += lower(0, ry, rx)
    go_back(0, low_part)
    back_zero = remote(
        back_out.at[0, z], back_in.at[core, z], back_near.at[0], back_near.at[2 + core],
        CORES * chip, far_side * NZ + z,
    )

    @pl.when(core == 1)
    def _():
        back_zero.start()

    @pl.when(core == 0)
    def _():
        pltpu.make_async_copy(
            back_out.at[0, z], back_in.at[core, z], back_near.at[2 + core]
        ).start()

    share_down(1)
    down_pair(1).wait_recv()
    high_part = lower(1, 0, 0)
    for ry, rx in order:
        high_part += lower(1, ry, rx)
    go_back(1, jnp.concatenate([low_part[:, own:], high_part], axis=1))
    back_one = remote(
        back_out.at[1, z], back_in.at[core, z], back_near.at[1], back_near.at[2 + core],
        CORES * chip + 1, far_side * NZ + z,
    )
    back_one.start()

    slots_all = slot_matrix(names, 0, total_slots)
    slots_now = jnp.where(
        side == 0, slots_all, jnp.concatenate([slots_all[half:], slots_all[:half]], axis=0)
    )
    pltpu.make_async_copy(
        weight_in.at[most_pipe], weight_in.at[most_pipe], weight_sem.at[1]
    ).wait()
    combining = jnp.transpose(slots_now) * weight_in[...].reshape(tok, total_slots)
    chip_tokens = tokens[:, block].astype(jnp.float32)
    padding = jnp.zeros((tok, 4 * LANES - own), jnp.float32)
    residual = jnp.where(
        core == 0, chip_tokens[:, : 4 * LANES],
        jnp.concatenate([chip_tokens[:, own:], padding], axis=1),
    )

    rows_left(len(PARTS) - 1)
    pltpu.make_async_copy(
        score_out.at[most_pipe], score_out.at[most_pipe], score_sem.at[0]
    ).wait()
    pltpu.make_async_copy(
        weight_in.at[most_pipe], weight_in.at[most_pipe], weight_sem.at[0]
    ).wait()
    for ry, rx in relative:
        down_to(0, ry, rx).wait_send()
        down_to(1, ry, rx).wait_send()
        hidden_to(ry, rx).wait_send()
    for copy in sent:
        copy.wait_send()
    gate_up_pair.wait_send()
    down_pair(0).wait_send()
    down_pair(1).wait_send()

    pltpu.make_async_copy(
        back_in.at[:, most], back_in.at[:, most], back_sem.at[1]
    ).wait()
    for k in range(HALVES):
        pltpu.make_async_copy(back_in.at[k, 0], back_in.at[k, 0], back_near.at[2 + k]).wait()
    returned = back_in[...].astype(jnp.float32)
    returned = jnp.concatenate(
        [
            returned[:, :, at * CAP : (at + 1) * CAP, :].reshape(total_slots, LANES)
            for at in range(4)
        ],
        axis=1,
    )
    mixed = residual + jnp.dot(
        combining, returned, preferred_element_type=jnp.float32, precision=lax.Precision.HIGHEST
    )
    out_ref[...] = jnp.transpose(mixed)[:own, :].astype(jnp.bfloat16)

    @pl.when(core == 1)
    def _():
        back_zero.wait_send()

    back_one.wait_send()
    pltpu.make_async_copy(back_out.at[:, most], back_out.at[:, most], back_sem.at[0]).wait()


def shards(tokens, norm_gain, router, routes, w_gate_up, w_down):
    tok, width = tokens.shape
    columns = width // CHIPS
    half = NZ * CAP
    units = w_down.shape[1]
    experts = router.shape[1]
    group = tok // PIPE
    bf16, f32 = jnp.bfloat16, jnp.float32
    dma = pltpu.SemaphoreType.DMA
    anywhere = pl.BlockSpec(memory_space=pl.ANY)
    vmem = pl.BlockSpec(memory_space=pltpu.VMEM)
    mixed = pl.pallas_call(
        kernel,
        out_shape=jax.ShapeDtypeStruct((width // PIPE, tok), bf16),
        in_specs=[anywhere, vmem, anywhere, vmem, anywhere, anywhere],
        out_specs=vmem,
        scratch_shapes=[
            pltpu.VMEM((tok, width), bf16),
            pltpu.VMEM((columns, experts), bf16),
            pltpu.VMEM((width, CORES * 2 * units), bf16),
            *[
                pltpu.VMEM((CHIPS, CORES, units, count * LANES), bf16)
                for _, count in DOWN_PARTS
            ],
            pltpu.VMEM((len(PARTS), NZ, PIECE, LANES), bf16),
            pltpu.VMEM((len(PARTS), NZ, PIECE, LANES), bf16),
            *[pltpu.VMEM((CHIPS, half, count * LANES), bf16) for _, count in PARTS],
            pltpu.VMEM((CHIPS, half, CORES * units), bf16),
            pltpu.VMEM((CORES, NZ, 32, LANES), bf16),
            pltpu.VMEM((HALVES, NZ, 32, LANES), bf16),
            pltpu.VMEM((PIPE, group, experts), f32),
            pltpu.VMEM((PIPE, group, experts), f32),
            pltpu.VMEM((group, 2 * half), f32),
            pltpu.VMEM((PIPE, group, 2 * half), f32),
            dma((8,)), dma((2 * len(PARTS),)), dma((2 * len(PARTS),)),
            dma((9 * len(PARTS),)), dma((2 * len(PARTS) * CHIPS,)), dma((6,)),
            dma((2, 2 * CHIPS)), dma((CHIPS,)), dma((CHIPS,)),
            dma((2,)), dma((4,)), dma((2,)), dma((2,)),
        ],
        compiler_params=pltpu.CompilerParams(
            collective_id=0, has_side_effects=True, vmem_limit_bytes=56 * 1024 * 1024
        ),
        cost_estimate=pl.CostEstimate(
            flops=2_000_000_000, bytes_accessed=8_000_000, transcendentals=100_000
        ),
    )(tokens, norm_gain.reshape(1, width), router, routes.T, w_gate_up, w_down)
    return mixed.T


def solution(mesh):
    placed = (
        P("ep", None),
        P(),
        P("pipe", None),
        P("ep", None),
        P("ep", None, "pipe"),
        P("ep", "pipe", None),
    )
    return jax.shard_map(
        shards, mesh=mesh, in_specs=placed, out_specs=P("ep", "pipe"), check_vma=False
    )
```

```python
import functools

import jax
import jax.numpy as jnp
from jax import lax
from jax.experimental import pallas as pl
from jax.experimental.pallas import tpu as pltpu
from jax.sharding import PartitionSpec as P

CORES = 2
NX = 4
NY = 2
CHIPS = NX * NY
PIPE = CHIPS * CORES
NZ = 16
HALVES = 2
CAP = 8
COLUMN_PARTS = ((0, 4), (4, 3))
PARTS = tuple((rows, first, count) for rows in (0, 1) for first, count in COLUMN_PARTS)
PIECE = 32
Y_FIRST = (0, 2)
ARRIVALS = (
    (0, 0, 0, None), (1, 0, 0, None), (0, 1, 0, None), (0, 0, 3, None), (0, 0, 1, None),
    (2, 0, 0, None), (1, 0, 3, None), (1, 0, 1, None), (1, 1, 0, None), (3, 0, 0, None),
    (0, 1, 3, None), (0, 1, 1, None), (2, 1, 0, None), (0, 0, 2, 0), (0, 0, 2, 1),
    (1, 1, 3, None), (2, 0, 1, None), (1, 1, 1, None), (1, 0, 2, 0), (1, 0, 2, 1),
    (2, 0, 3, None), (3, 1, 0, None), (3, 0, 3, None), (3, 0, 1, None), (1, 1, 2, 0),
    (1, 1, 2, 1), (0, 1, 2, 0), (0, 1, 2, 1), (2, 1, 3, None), (2, 1, 1, None),
    (2, 0, 2, 0), (2, 0, 2, 1), (3, 1, 3, None), (3, 0, 2, 0), (3, 0, 2, 1),
    (3, 1, 1, None), (2, 1, 2, 0), (2, 1, 2, 1), (3, 1, 2, 0), (3, 1, 2, 1),
)
DOWN_FROM, FIRST_HIDDEN, FIRST_RETURN = 3, 27, 34
LANES = 128
MESH = pl.DeviceIdType.MESH


def remote(src, dst, send, recv, pipe, ep):
    return pltpu.make_async_remote_copy(
        src_ref=src,
        dst_ref=dst,
        send_sem=send,
        recv_sem=recv,
        device_id=(pipe, ep),
        device_id_type=MESH,
    )


def one_hot(names, first, count, width):
    row = lax.broadcasted_iota(jnp.int32, (width, names.shape[1]), 0)
    expert = first + row // count
    named = names[0:1, :] == expert
    for k in range(1, names.shape[0]):
        named = named | (names[k : k + 1, :] == expert)
    return jnp.where(named, 1.0, 0.0), row


def slot_matrix(names, first, width):
    named, row = one_hot(names, first, CAP, width)
    tok = names.shape[1]
    earlier = lax.broadcasted_iota(jnp.int32, (tok, tok), 0) < lax.broadcasted_iota(
        jnp.int32, (tok, tok), 1
    )
    rank = jnp.dot(
        named.astype(jnp.bfloat16),
        jnp.where(earlier, 1.0, 0.0).astype(jnp.bfloat16),
        preferred_element_type=jnp.float32,
    )
    return jnp.where(rank == (row % CAP).astype(jnp.float32), named, 0.0)


def kernel(
    tokens_hbm, gain_ref, router_hbm, routes_ref, gate_up_hbm, down_hbm, out_ref,
    tokens, router, gate_up, down_a, down_b,
    outbox, inbox, rows_a, rows_b, rows_c, rows_d, hidden, back_out, back_in,
    score_out, score_in, weight_out, weight_in,
    load_sem, near_sem, out_sem, gather_send, gather_recv, pair_sem,
    down_sem, hidden_send, hidden_recv, back_sem, back_near,
    score_sem, weight_sem,
):
    pipe, ep = lax.axis_index("pipe"), lax.axis_index("ep")
    core, chip = lax.rem(pipe, CORES), lax.div(pipe, CORES)
    x, y = lax.rem(chip, NX), lax.div(chip, NX)
    z, side = lax.rem(ep, NZ), lax.div(ep, NZ)
    far_side = lax.rem(side + core, HALVES)
    partner = pipe + 1 - 2 * core
    tok, width = tokens.shape
    columns = width // CHIPS
    tiles = columns // LANES
    half = NZ * CAP
    own = columns // CORES
    units = down_a.shape[2]
    parity = lax.rem(z, 2)
    span = half // 2
    downs = (down_a, down_b)
    total_slots = HALVES * half

    def column_block(which):
        return pl.ds(pl.multiple_of(which * columns, LANES), columns)

    def down_columns(part, which):
        first, count = COLUMN_PARTS[part]
        start = pl.multiple_of(which * columns + first * LANES, LANES)
        return down_hbm.at[0, :, pl.ds(start, count * LANES)]

    def far_first(i):
        return lax.rem(z + NZ // 2 + lax.div(i, 2) * (1 - 2 * lax.rem(i, 2)), NZ)

    own_lanes = pl.ds(pl.multiple_of(core * 2 * units, LANES), 2 * units)
    quarter = width // 4
    token_loads = [
        pltpu.make_async_copy(
            tokens_hbm.at[:, pl.ds(n * quarter, quarter)],
            tokens.at[:, pl.ds(n * quarter, quarter)],
            load_sem.at[4 + n],
        )
        for n in range(4)
    ]
    for load in token_loads:
        load.start()

    barrier = pltpu.get_barrier_semaphore()

    def greet_pipe(i, _):
        pl.semaphore_signal(
            barrier, inc=1, device_id=(lax.rem(pipe + i, PIPE), ep), device_id_type=MESH
        )
        return 0

    lax.fori_loop(1, PIPE, greet_pipe, 0)

    def greet_ep(i, _):
        other = lax.rem(z + i, NZ)
        for k in range(CORES):
            pl.semaphore_signal(
                barrier, inc=1,
                device_id=(CORES * chip + k, lax.rem(side + k, HALVES) * NZ + other),
                device_id_type=MESH,
            )
        return 0

    lax.fori_loop(1, NZ, greet_ep, 0)
    pl.semaphore_signal(
        barrier, inc=1,
        device_id=(CORES * chip + 1, (1 - side) * NZ + z), device_id_type=MESH,
    )

    @pl.when(core == 1)
    def _():
        pl.semaphore_signal(barrier, inc=1, device_id=(partner, ep), device_id_type=MESH)

    names = routes_ref[...]
    placing = slot_matrix(names, lax.rem(core + side, HALVES) * NZ, half).astype(jnp.bfloat16)

    squares = jnp.zeros((tok, LANES), jnp.float32)
    for n in range(4):
        token_loads[n].wait()
        for at in range(n * quarter // LANES, (n + 1) * quarter // LANES):
            values = tokens[:, at * LANES : (at + 1) * LANES].astype(jnp.float32)
            squares += values * values
    router[...] = jnp.zeros_like(router)
    loads = [
        pltpu.make_async_copy(src, dst, load_sem.at[number])
        for number, (src, dst) in enumerate(
            ((router_hbm, router.at[pl.ds(core * own, own), :]),
             (gate_up_hbm.at[0], gate_up.at[:, own_lanes]),
             (down_columns(0, chip), down_a.at[chip, core]),
             (down_columns(1, chip), down_b.at[chip, core]))
        )
    ]
    for load in loads:
        load.start()
    scale = lax.rsqrt(jnp.sum(squares, axis=1, keepdims=True) / width + 1e-06)
    block = column_block(chip)
    normed = (tokens[:, block].astype(jnp.float32) * scale * gain_ref[:, block]).astype(
        jnp.bfloat16
    )
    placed = jnp.dot(placing, normed, preferred_element_type=jnp.float32)
    for part, (first, count) in enumerate(COLUMN_PARTS):
        pieces = [
            placed[:, at * LANES : (at + 1) * LANES].reshape(NZ, CAP, LANES)
            for at in range(first, first + count)
        ]
        if count * CAP < PIECE:
            pieces.append(jnp.zeros((NZ, PIECE - count * CAP, LANES), jnp.float32))
        outbox[part] = jnp.concatenate(pieces, axis=1).astype(jnp.bfloat16)

    pl.semaphore_wait(barrier, PIPE - 1 + 2 * NZ - 1 + core)

    def near_copy(part):
        return remote(
            outbox.at[part, z], inbox.at[parity, part, lax.div(z, 2)],
            near_sem.at[part], near_sem.at[2 + part], pipe, far_side * NZ + z,
        )

    def send_rows(part):
        def dispatch(i, _):
            other = far_first(i)
            remote(
                outbox.at[part, other], inbox.at[parity, part, lax.div(z, 2)],
                out_sem.at[part], out_sem.at[2 + 2 * parity + part],
                pipe, far_side * NZ + other,
            ).start()
            return 0

        lax.fori_loop(1, NZ, dispatch, 0)

        @pl.when(core == 1)
        def _():
            near_copy(part).start()

        @pl.when(core == 0)
        def _():
            pltpu.make_async_copy(
                outbox.at[part, z], inbox.at[parity, part, lax.div(z, 2)], near_sem.at[2 + part]
            ).start()

    def rows_left(part):
        pltpu.make_async_copy(
            outbox.at[part, most], outbox.at[part, most], out_sem.at[part]
        ).wait()

        @pl.when(core == 1)
        def _():
            near_copy(part).wait_send()

    most = pl.ds(0, NZ - 1)

    @pl.when(parity == 0)
    def _():
        send_rows(0)

    def chip_at(ry, rx):
        return lax.rem(y + ry, NY) * NX + lax.rem(x + rx, NX)

    relative = [(ry, rx) for rx in (2, 1, 3, 0) for ry in (1, 0) if (ry, rx) != (0, 0)]
    mirror = {(ry, rx): ry * NX + (NX - rx) % NX for ry, rx in relative}

    def down_to(part, ry, rx):
        return remote(
            down_columns(part, chip_at(ry, rx)), downs[part].at[chip, core],
            down_sem.at[part, ry * NX + rx], down_sem.at[part, CHIPS + mirror[ry, rx]],
            CORES * chip_at(ry, rx) + core, ep,
        )

    def down_pair(part):
        return remote(
            downs[part].at[:, core], downs[part].at[:, core],
            pair_sem.at[2 + 2 * part], pair_sem.at[3 + 2 * part], partner, ep,
        )

    def share_down(part):
        loads[2 + part].wait()
        for ry, rx in relative:
            down_to(part, ry, rx).wait_recv()
        down_pair(part).start()

    for ry, rx in relative:
        down_to(0, ry, rx).start()
    gate_up_pair = remote(
        gate_up_hbm.at[0], gate_up.at[:, own_lanes], pair_sem.at[0], pair_sem.at[1], partner, ep
    )
    gate_up_pair.start()

    loads[0].wait()
    scores = jnp.dot(normed, router[...], preferred_element_type=jnp.float32)
    score_out[...] = scores.reshape(score_out.shape)
    score_in[pipe] = score_out[pipe]

    def send_scores(i, _):
        other = lax.rem(pipe + i, PIPE)
        remote(
            score_out.at[other], score_in.at[pipe], score_sem.at[0], score_sem.at[1], other, ep
        ).start()
        return 0

    lax.fori_loop(1, PIPE, send_scores, 0)

    @pl.when(parity == 0)
    def _():
        rows_left(0)
        send_rows(1)

    gathered = (rows_a, rows_b, rows_c, rows_d)
    sent = []

    def arrive(part):
        rows_half, _, count = PARTS[part]
        column_part = part % 2
        box = inbox.at[rows_half, column_part]
        others = box.at[pl.ds(0, NZ // 2 - 1)]

        @pl.when(parity == rows_half)
        def _():
            pltpu.make_async_copy(others, others, out_sem.at[2 + part]).wait()
            pltpu.make_async_copy(box.at[0], box.at[0], near_sem.at[2 + column_part]).wait()

        @pl.when(parity != rows_half)
        def _():
            pltpu.make_async_copy(box, box, out_sem.at[2 + part]).wait()
            if rows_half == 0:
                if column_part == 1:
                    rows_left(0)
                send_rows(column_part)

        arrived = inbox[rows_half, column_part].astype(jnp.float32)
        for at in range(count):
            gathered[part][chip, :, at * LANES : (at + 1) * LANES] = (
                arrived[:, at * CAP : (at + 1) * CAP, :].reshape(span, LANES).astype(jnp.bfloat16)
            )

    def block_ref(part, ry, rx, piece):
        ref = gathered[part].at[chip_at(ry, rx)]
        return ref if piece is None else ref.at[pl.ds(piece * (span // 2), span // 2), :]

    def recv_sem(part, ry, rx, piece):
        return gather_recv.at[(part * CHIPS + (ry % NY) * NX + rx % NX) * 2 + (piece or 0)]

    def pass_on(part, block, target, piece=None):
        (ry, rx), (ty, tx) = block, target
        ref = block_ref(part, ry, rx, piece)
        copy = remote(
            ref, ref, gather_send.at[len(sent)], recv_sem(part, ry + ty, rx - tx + NX, piece),
            CORES * chip_at(ty, tx) + core, ep,
        )
        copy.start()
        sent.append(copy)

    def take(part, ry, rx, piece=None):
        ref = block_ref(part, ry, rx, piece)
        pltpu.make_async_copy(ref, ref, recv_sem(part, ry, rx, piece)).wait()

    up, plus, minus = (1, 0), (0, 1), (0, 3)

    def project(part, ry, rx):
        _, first, count = PARTS[part]
        which = chip_at(ry, rx)
        start = pl.multiple_of(which * columns + first * LANES, LANES)
        return jnp.dot(
            gathered[part][which], gate_up[pl.ds(start, count * LANES), :],
            preferred_element_type=jnp.float32,
        )

    def hidden_to(rows_half, ry, rx):
        ref = hidden.at[rows_half, chip]
        return remote(
            ref, ref, hidden_send.at[rows_half, ry * NX + rx],
            hidden_recv.at[rows_half, mirror[ry, rx]],
            CORES * chip_at(ry, rx) + core, ep,
        )

    def send_hidden(rows_half, both):
        parts = []
        for k in range(CORES):
            gate = both[:, 2 * k * units : (2 * k + 1) * units]
            upper = both[:, (2 * k + 1) * units : (2 * k + 2) * units]
            parts.append(gate / (1.0 + jnp.exp(-gate)) * upper)
        hidden[rows_half, chip] = jnp.concatenate(parts, axis=1).astype(jnp.bfloat16)
        for ry, rx in relative:
            hidden_to(rows_half, ry, rx).start()

    order = [(1, 0), (0, 1), (0, 3), (1, 1), (1, 3), (0, 2), (1, 2)]

    def lower(rows_half, part, ry, rx):
        which = chip_at(ry, rx)
        return jnp.dot(
            hidden[rows_half, which],
            downs[part][which].reshape(CORES * units, COLUMN_PARTS[part][1] * LANES),
            preferred_element_type=jnp.float32,
        )

    def send_back(rows_half, j, result):
        pieces = []
        for at in range(4):
            low, high = at * LANES, min((at + 1) * LANES, own)
            piece = result[:, low:high]
            if high - low < LANES:
                piece = jnp.concatenate(
                    [piece, jnp.zeros((span, LANES - (high - low)), jnp.float32)], axis=1
                )
            pieces.append(piece.reshape(NZ // 2, CAP, LANES))
        back_out[rows_half, j] = jnp.concatenate(pieces, axis=1).astype(jnp.bfloat16)
        apart = lax.rem(parity + rows_half, 2)

        def send(steps):
            other = lax.rem(z + 2 * steps + apart, NZ)
            remote(
                back_out.at[rows_half, j, lax.div(other, 2)], back_in.at[core, z],
                back_sem.at[0], back_sem.at[1],
                CORES * chip + j, far_side * NZ + other,
            ).start()

        def go(i, _):
            send(NZ // 4 + lax.div(i, 2) * (1 - 2 * lax.rem(i, 2)))
            return 0

        lax.fori_loop(1, NZ // 2, go, 0)

        @pl.when(apart == 1)
        def _():
            send(0)

    def finish(rows_half):
        low_part = lower(rows_half, 0, 0, 0)
        for ry, rx in order:
            hidden_to(rows_half, ry, (NX - rx) % NX).wait_recv()
            low_part += lower(rows_half, 0, ry, rx)
        send_back(rows_half, 0, low_part)
        high_part = lower(rows_half, 1, 0, 0)
        for ry, rx in order:
            high_part += lower(rows_half, 1, ry, rx)
        send_back(rows_half, 1, jnp.concatenate([low_part[:, own:], high_part], axis=1))

    both = [jnp.zeros((span, CORES * 2 * units), jnp.float32) for _ in range(2)]
    for step, (part, ry, rx, piece) in enumerate(ARRIVALS):
        here = (ry, rx)
        if here == (0, 0):
            arrive(part)
            for target in (up, plus, minus) if part in Y_FIRST else (plus, minus, up):
                pass_on(part, here, target)
        else:
            take(part, ry, rx, piece)
            if part in Y_FIRST:
                if here == up:
                    pass_on(part, here, plus)
                    pass_on(part, here, minus)
            elif ry == 0 and rx == 2:
                pass_on(part, here, up, piece)
            if part in Y_FIRST or ry == 0:
                if rx == 3:
                    pass_on(part, here, plus, 0)
                elif rx == 1:
                    pass_on(part, here, minus, 1)
            if part not in Y_FIRST and ry == 0 and rx != 2:
                pass_on(part, here, up)
        if step == 0:
            loads[1].wait()
            gate_up_pair.wait_recv()
        if DOWN_FROM <= step < DOWN_FROM + len(relative):
            down_to(1, *relative[step - DOWN_FROM]).start()
        if (part, ry, rx) == (2, 0, 0):
            share_down(0)
        if piece != 0:
            both[part // 2] += project(part, ry, rx)
        if step == FIRST_HIDDEN:
            send_hidden(0, both[0])
            share_down(1)
        if step == FIRST_RETURN:
            down_pair(0).wait_recv()
            down_pair(1).wait_recv()
            finish(0)
    send_hidden(1, both[1])
    finish(1)

    back_near_out = back_out.at[parity]
    back_zero = remote(
        back_near_out.at[0, lax.div(z, 2)], back_in.at[core, z],
        back_near.at[0], back_near.at[2 + core], CORES * chip, far_side * NZ + z,
    )
    back_one = remote(
        back_near_out.at[1, lax.div(z, 2)], back_in.at[core, z],
        back_near.at[1], back_near.at[2 + core], CORES * chip + 1, far_side * NZ + z,
    )
    back_one.start()

    @pl.when(core == 1)
    def _():
        back_zero.start()

    @pl.when(core == 0)
    def _():
        pltpu.make_async_copy(
            back_near_out.at[0, lax.div(z, 2)], back_in.at[core, z], back_near.at[2 + core]
        ).start()

    most_pipe = pl.ds(0, PIPE - 1)
    pltpu.make_async_copy(score_in.at[most_pipe], score_in.at[most_pipe], score_sem.at[1]).wait()
    affinity = jax.nn.sigmoid(jnp.sum(score_in[...], axis=0))
    group, experts = affinity.shape
    pick_token = lax.broadcasted_iota(jnp.int32, (group, tok), 1)
    pick_row = lax.broadcasted_iota(jnp.int32, (group, tok), 0)
    pick = jnp.where(pick_token == pick_row + pipe * group, 1.0, 0.0).astype(jnp.bfloat16)
    chosen_all, _ = one_hot(names, 0, 1, experts)
    chosen = lax.dot_general(
        pick, chosen_all.astype(jnp.bfloat16), (((1,), (1,)), ((), ())),
        preferred_element_type=jnp.float32,
    )
    fraction = 2.5 * affinity / jnp.sum(chosen * affinity, axis=1, keepdims=True)
    spread_row = lax.broadcasted_iota(jnp.int32, (experts, total_slots), 0)
    spread_lane = lax.broadcasted_iota(jnp.int32, (experts, total_slots), 1)
    slot_expert = lax.rem(spread_lane // CAP + side * NZ, HALVES * NZ)
    weight_out[...] = jnp.dot(
        fraction, jnp.where(spread_row == slot_expert, 1.0, 0.0),
        preferred_element_type=jnp.float32, precision=lax.Precision.HIGHEST,
    )
    weight_in[pipe] = weight_out[...]

    def send_weights(i, _):
        other = lax.rem(pipe + i, PIPE)
        remote(weight_out, weight_in.at[pipe], weight_sem.at[0], weight_sem.at[1], other, ep).start()
        return 0

    lax.fori_loop(1, PIPE, send_weights, 0)

    slots_all = slot_matrix(names, 0, total_slots)
    slots_now = jnp.where(
        side == 0, slots_all, jnp.concatenate([slots_all[half:], slots_all[:half]], axis=0)
    )
    pltpu.make_async_copy(
        weight_in.at[most_pipe], weight_in.at[most_pipe], weight_sem.at[1]
    ).wait()
    combining = jnp.transpose(slots_now) * weight_in[...].reshape(tok, total_slots)
    chip_tokens = tokens[:, block].astype(jnp.float32)
    padding = jnp.zeros((tok, 4 * LANES - own), jnp.float32)
    residual = jnp.where(
        core == 0, chip_tokens[:, : 4 * LANES],
        jnp.concatenate([chip_tokens[:, own:], padding], axis=1),
    )

    rows_left(1)
    pltpu.make_async_copy(
        score_out.at[most_pipe], score_out.at[most_pipe], score_sem.at[0]
    ).wait()
    pltpu.make_async_copy(
        weight_in.at[most_pipe], weight_in.at[most_pipe], weight_sem.at[0]
    ).wait()
    for ry, rx in relative:
        down_to(0, ry, rx).wait_send()
        down_to(1, ry, rx).wait_send()
        hidden_to(0, ry, rx).wait_send()
        hidden_to(1, ry, rx).wait_send()
    for copy in sent:
        copy.wait_send()
    gate_up_pair.wait_send()
    down_pair(0).wait_send()
    down_pair(1).wait_send()

    pltpu.make_async_copy(
        back_in.at[:, most], back_in.at[:, most], back_sem.at[1]
    ).wait()
    for k in range(HALVES):
        pltpu.make_async_copy(back_in.at[k, 0], back_in.at[k, 0], back_near.at[2 + k]).wait()
    returned = back_in[...].astype(jnp.float32)
    returned = jnp.concatenate(
        [
            returned[:, :, at * CAP : (at + 1) * CAP, :].reshape(total_slots, LANES)
            for at in range(4)
        ],
        axis=1,
    )
    mixed = residual + jnp.dot(
        combining, returned, preferred_element_type=jnp.float32, precision=lax.Precision.HIGHEST
    )
    out_ref[...] = jnp.transpose(mixed)[:own, :].astype(jnp.bfloat16)

    @pl.when(core == 1)
    def _():
        back_zero.wait_send()

    back_one.wait_send()
    pltpu.make_async_copy(back_in.at[:, most], back_in.at[:, most], back_sem.at[0]).wait()


def shards(tokens, norm_gain, router, routes, w_gate_up, w_down):
    tok, width = tokens.shape
    columns = width // CHIPS
    half = NZ * CAP
    units = w_down.shape[1]
    experts = router.shape[1]
    group = tok // PIPE
    bf16, f32 = jnp.bfloat16, jnp.float32
    dma = pltpu.SemaphoreType.DMA
    anywhere = pl.BlockSpec(memory_space=pl.ANY)
    vmem = pl.BlockSpec(memory_space=pltpu.VMEM)
    mixed = pl.pallas_call(
        kernel,
        out_shape=jax.ShapeDtypeStruct((width // PIPE, tok), bf16),
        in_specs=[anywhere, vmem, anywhere, vmem, anywhere, anywhere],
        out_specs=vmem,
        scratch_shapes=[
            pltpu.VMEM((tok, width), bf16),
            pltpu.VMEM((columns, experts), bf16),
            pltpu.VMEM((width, CORES * 2 * units), bf16),
            *[
                pltpu.VMEM((CHIPS, CORES, units, count * LANES), bf16)
                for _, count in COLUMN_PARTS
            ],
            pltpu.VMEM((len(COLUMN_PARTS), NZ, PIECE, LANES), bf16),
            pltpu.VMEM((2, len(COLUMN_PARTS), NZ // 2, PIECE, LANES), bf16),
            *[pltpu.VMEM((CHIPS, half // 2, count * LANES), bf16) for _, _, count in PARTS],
            pltpu.VMEM((2, CHIPS, half // 2, CORES * units), bf16),
            pltpu.VMEM((2, CORES, NZ // 2, 32, LANES), bf16),
            pltpu.VMEM((HALVES, NZ, 32, LANES), bf16),
            pltpu.VMEM((PIPE, group, experts), f32),
            pltpu.VMEM((PIPE, group, experts), f32),
            pltpu.VMEM((group, 2 * half), f32),
            pltpu.VMEM((PIPE, group, 2 * half), f32),
            dma((8,)), dma((4,)), dma((6,)),
            dma((9 * len(PARTS),)), dma((2 * len(PARTS) * CHIPS,)), dma((6,)),
            dma((2, 2 * CHIPS)), dma((2, CHIPS)), dma((2, CHIPS)),
            dma((2,)), dma((4,)), dma((2,)), dma((2,)),
        ],
        compiler_params=pltpu.CompilerParams(
            collective_id=0, has_side_effects=True, vmem_limit_bytes=56 * 1024 * 1024
        ),
        cost_estimate=pl.CostEstimate(
            flops=2_000_000_000, bytes_accessed=8_000_000, transcendentals=100_000
        ),
    )(tokens, norm_gain.reshape(1, width), router, routes.T, w_gate_up, w_down)
    return mixed.T


def solution(mesh):
    placed = (
        P("ep", None),
        P(),
        P("pipe", None),
        P("ep", None),
        P("ep", None, "pipe"),
        P("ep", "pipe", None),
    )
    return jax.shard_map(
        shards, mesh=mesh, in_specs=placed, out_specs=P("ep", "pipe"), check_vma=False
    )
```

```python
import functools

import jax
import jax.numpy as jnp
from jax import lax
from jax.experimental import pallas as pl
from jax.experimental.pallas import tpu as pltpu
from jax.sharding import PartitionSpec as P

CORES = 2
NX = 4
NY = 2
CHIPS = NX * NY
PIPE = CHIPS * CORES
NZ = 16
HALVES = 2
CAP = 8
COLUMN_PARTS = ((0, 4), (4, 3))
PARTS = tuple((rows, first, count) for rows in (0, 1) for first, count in COLUMN_PARTS)
PIECE = 32
Y_FIRST = (1, 2)
ARRIVALS = (
    (0, 0, 0, None), (1, 0, 0, None), (0, 0, 3, None), (0, 0, 1, None), (0, 1, 0, None),
    (2, 0, 0, None), (1, 0, 3, None), (1, 0, 1, None), (1, 1, 0, None), (0, 0, 2, 0),
    (0, 0, 2, 1), (0, 1, 3, None), (3, 0, 0, None), (2, 0, 3, None), (2, 0, 1, None),
    (1, 0, 2, 0), (1, 0, 2, 1), (0, 1, 1, None), (1, 1, 3, None), (1, 1, 1, None),
    (2, 1, 0, None), (3, 0, 1, None), (0, 1, 2, 0), (2, 0, 2, 1), (0, 1, 2, 1),
    (3, 0, 3, None), (2, 0, 2, 0), (1, 1, 2, 0), (1, 1, 2, 1), (3, 1, 0, None),
    (2, 1, 3, None), (2, 1, 1, None), (3, 0, 2, 1), (3, 0, 2, 0), (2, 1, 2, 0),
    (2, 1, 2, 1), (3, 1, 1, None), (3, 1, 3, None), (3, 1, 2, 1), (3, 1, 2, 0),
)
DOWN_FROM, FIRST_HIDDEN, FIRST_RETURN = 9, 28, 33
LANES = 128
MESH = pl.DeviceIdType.MESH


def mod(value, size):
    return value & (size - 1)


def quotient(value, size):
    return value >> (size.bit_length() - 1)


def remote(src, dst, send, recv, pipe, ep):
    return pltpu.make_async_remote_copy(
        src_ref=src,
        dst_ref=dst,
        send_sem=send,
        recv_sem=recv,
        device_id=(pipe, ep),
        device_id_type=MESH,
    )


def one_hot(names, first, count, width):
    row = lax.broadcasted_iota(jnp.int32, (width, names.shape[1]), 0)
    expert = first + row // count
    named = names[0:1, :] == expert
    for k in range(1, names.shape[0]):
        named = named | (names[k : k + 1, :] == expert)
    return jnp.where(named, 1.0, 0.0), row


def slot_matrix(names, first, width):
    named, row = one_hot(names, first, CAP, width)
    tok = names.shape[1]
    earlier = lax.broadcasted_iota(jnp.int32, (tok, tok), 0) < lax.broadcasted_iota(
        jnp.int32, (tok, tok), 1
    )
    rank = jnp.dot(
        named.astype(jnp.bfloat16),
        jnp.where(earlier, 1.0, 0.0).astype(jnp.bfloat16),
        preferred_element_type=jnp.float32,
    )
    return jnp.where(rank == (row % CAP).astype(jnp.float32), named, 0.0)


def kernel(
    tokens_hbm, gain_ref, router_hbm, routes_ref, gate_up_hbm, down_hbm, out_ref,
    tokens, router, gate_up, down_a, down_b,
    outbox, inbox, rows_a, rows_b, rows_c, rows_d, hidden, back_out, back_in,
    score_out, score_in, weight_out, weight_in,
    load_sem, near_sem, out_sem, gather_send, gather_recv, pair_sem,
    down_sem, hidden_send, hidden_recv, back_sem, back_near,
    score_sem, weight_sem,
):
    pipe, ep = lax.axis_index("pipe"), lax.axis_index("ep")
    core, chip = mod(pipe, CORES), quotient(pipe, CORES)
    x, y = mod(chip, NX), quotient(chip, NX)
    z, side = mod(ep, NZ), quotient(ep, NZ)
    far_side = mod(side + core, HALVES)
    partner = pipe + 1 - 2 * core
    tok, width = tokens.shape
    columns = width // CHIPS
    tiles = columns // LANES
    half = NZ * CAP
    own = columns // CORES
    units = down_a.shape[2]
    parity = mod(z, 2)
    span = half // 2
    downs = (down_a, down_b)
    total_slots = HALVES * half

    def column_block(which):
        return pl.ds(pl.multiple_of(which * columns, LANES), columns)

    def down_columns(part, which):
        first, count = COLUMN_PARTS[part]
        start = pl.multiple_of(which * columns + first * LANES, LANES)
        return down_hbm.at[0, :, pl.ds(start, count * LANES)]

    def far_first(i):
        return mod(z + NZ // 2 + quotient(i, 2) * (1 - 2 * mod(i, 2)), NZ)

    own_lanes = pl.ds(pl.multiple_of(core * 2 * units, LANES), 2 * units)
    quarter = width // 4
    token_loads = [
        pltpu.make_async_copy(
            tokens_hbm.at[:, pl.ds(n * quarter, quarter)],
            tokens.at[:, pl.ds(n * quarter, quarter)],
            load_sem.at[4 + n],
        )
        for n in range(4)
    ]
    for load in token_loads:
        load.start()

    barrier = pltpu.get_barrier_semaphore()

    def greet_pipe(i, _):
        pl.semaphore_signal(
            barrier, inc=1, device_id=(mod(pipe + i, PIPE), ep), device_id_type=MESH
        )
        return 0

    lax.fori_loop(1, PIPE, greet_pipe, 0)

    def greet_ep(i, _):
        other = mod(z + i, NZ)
        for k in range(CORES):
            pl.semaphore_signal(
                barrier, inc=1,
                device_id=(CORES * chip + k, mod(side + k, HALVES) * NZ + other),
                device_id_type=MESH,
            )
        return 0

    lax.fori_loop(1, NZ, greet_ep, 0)
    pl.semaphore_signal(
        barrier, inc=1,
        device_id=(CORES * chip + 1, (1 - side) * NZ + z), device_id_type=MESH,
    )

    @pl.when(core == 1)
    def _():
        pl.semaphore_signal(barrier, inc=1, device_id=(partner, ep), device_id_type=MESH)

    names = routes_ref[...]
    placing = slot_matrix(names, mod(core + side, HALVES) * NZ, half).astype(jnp.bfloat16)

    squares = jnp.zeros((tok, LANES), jnp.float32)
    for n in range(4):
        token_loads[n].wait()
        for at in range(n * quarter // LANES, (n + 1) * quarter // LANES):
            values = tokens[:, at * LANES : (at + 1) * LANES].astype(jnp.float32)
            squares += values * values
    router[...] = jnp.zeros_like(router)
    loads = [
        pltpu.make_async_copy(src, dst, load_sem.at[number])
        for number, (src, dst) in enumerate(
            ((router_hbm, router.at[pl.ds(core * own, own), :]),
             (gate_up_hbm.at[0], gate_up.at[:, own_lanes]),
             (down_columns(0, chip), down_a.at[chip, core]),
             (down_columns(1, chip), down_b.at[chip, core]))
        )
    ]
    for load in loads:
        load.start()
    scale = lax.rsqrt(jnp.sum(squares, axis=1, keepdims=True) / width + 1e-06)
    block = column_block(chip)
    normed = (tokens[:, block].astype(jnp.float32) * scale * gain_ref[:, block]).astype(
        jnp.bfloat16
    )
    placed = jnp.dot(placing, normed, preferred_element_type=jnp.float32)
    for part, (first, count) in enumerate(COLUMN_PARTS):
        pieces = [
            placed[:, at * LANES : (at + 1) * LANES].reshape(NZ, CAP, LANES)
            for at in range(first, first + count)
        ]
        if count * CAP < PIECE:
            pieces.append(jnp.zeros((NZ, PIECE - count * CAP, LANES), jnp.float32))
        outbox[part] = jnp.concatenate(pieces, axis=1).astype(jnp.bfloat16)

    pl.semaphore_wait(barrier, PIPE - 1 + 2 * NZ - 1 + core)

    def near_copy(part):
        return remote(
            outbox.at[part, z], inbox.at[parity, part, quotient(z, 2)],
            near_sem.at[part], near_sem.at[2 + part], pipe, far_side * NZ + z,
        )

    def send_rows(part):
        for i in range(1, NZ):
            other = far_first(i)
            remote(
                outbox.at[part, other], inbox.at[parity, part, quotient(z, 2)],
                out_sem.at[part], out_sem.at[2 + 2 * parity + part],
                pipe, far_side * NZ + other,
            ).start()

        @pl.when(core == 1)
        def _():
            near_copy(part).start()

        @pl.when(core == 0)
        def _():
            pltpu.make_async_copy(
                outbox.at[part, z], inbox.at[parity, part, quotient(z, 2)], near_sem.at[2 + part]
            ).start()

    def rows_left(part):
        pltpu.make_async_copy(
            outbox.at[part, most], outbox.at[part, most], out_sem.at[part]
        ).wait()

        @pl.when(core == 1)
        def _():
            near_copy(part).wait_send()

    most = pl.ds(0, NZ - 1)

    @pl.when(parity == 0)
    def _():
        send_rows(0)

    def chip_at(ry, rx):
        return mod(y + ry, NY) * NX + mod(x + rx, NX)

    relative = [(ry, rx) for rx in (2, 1, 3, 0) for ry in (1, 0) if (ry, rx) != (0, 0)]
    mirror = {(ry, rx): ry * NX + (NX - rx) % NX for ry, rx in relative}

    def down_to(part, ry, rx):
        return remote(
            down_columns(part, chip_at(ry, rx)), downs[part].at[chip, core],
            down_sem.at[part, ry * NX + rx], down_sem.at[part, CHIPS + mirror[ry, rx]],
            CORES * chip_at(ry, rx) + core, ep,
        )

    def down_pair(part):
        return remote(
            downs[part].at[:, core], downs[part].at[:, core],
            pair_sem.at[2 + 2 * part], pair_sem.at[3 + 2 * part], partner, ep,
        )

    def share_down(part):
        loads[2 + part].wait()
        for ry, rx in relative:
            down_to(part, ry, rx).wait_recv()
        down_pair(part).start()

    for ry, rx in relative:
        down_to(0, ry, rx).start()
    gate_up_pair = remote(
        gate_up_hbm.at[0], gate_up.at[:, own_lanes], pair_sem.at[0], pair_sem.at[1], partner, ep
    )
    gate_up_pair.start()

    loads[0].wait()
    scores = jnp.dot(normed, router[...], preferred_element_type=jnp.float32)
    score_out[...] = scores.reshape(score_out.shape)
    score_in[pipe] = score_out[pipe]

    def send_scores(i, _):
        other = mod(pipe + i, PIPE)
        remote(
            score_out.at[other], score_in.at[pipe], score_sem.at[0], score_sem.at[1], other, ep
        ).start()
        return 0

    lax.fori_loop(1, PIPE, send_scores, 0)

    @pl.when(parity == 0)
    def _():
        rows_left(0)
        send_rows(1)

    gathered = (rows_a, rows_b, rows_c, rows_d)
    sent = []

    def arrive(part):
        rows_half, _, count = PARTS[part]
        column_part = part % 2
        box = inbox.at[rows_half, column_part]
        others = box.at[pl.ds(0, NZ // 2 - 1)]

        @pl.when(parity == rows_half)
        def _():
            pltpu.make_async_copy(others, others, out_sem.at[2 + part]).wait()
            pltpu.make_async_copy(box.at[0], box.at[0], near_sem.at[2 + column_part]).wait()

        @pl.when(parity != rows_half)
        def _():
            pltpu.make_async_copy(box, box, out_sem.at[2 + part]).wait()
            if rows_half == 0:
                if column_part == 1:
                    rows_left(0)
                send_rows(column_part)

        arrived = inbox[rows_half, column_part].astype(jnp.float32)
        for at in range(count):
            gathered[part][chip, :, at * LANES : (at + 1) * LANES] = (
                arrived[:, at * CAP : (at + 1) * CAP, :].reshape(span, LANES).astype(jnp.bfloat16)
            )

    def block_ref(part, ry, rx, piece):
        ref = gathered[part].at[chip_at(ry, rx)]
        return ref if piece is None else ref.at[pl.ds(piece * (span // 2), span // 2), :]

    def recv_sem(part, ry, rx, piece):
        return gather_recv.at[(part * CHIPS + (ry % NY) * NX + rx % NX) * 2 + (piece or 0)]

    def pass_on(part, block, target, piece=None):
        (ry, rx), (ty, tx) = block, target
        ref = block_ref(part, ry, rx, piece)
        copy = remote(
            ref, ref, gather_send.at[len(sent)], recv_sem(part, ry + ty, rx - tx + NX, piece),
            CORES * chip_at(ty, tx) + core, ep,
        )
        copy.start()
        sent.append(copy)

    def take(part, ry, rx, piece=None):
        ref = block_ref(part, ry, rx, piece)
        pltpu.make_async_copy(ref, ref, recv_sem(part, ry, rx, piece)).wait()

    up, plus, minus = (1, 0), (0, 1), (0, 3)

    def project(part, ry, rx):
        _, first, count = PARTS[part]
        which = chip_at(ry, rx)
        start = pl.multiple_of(which * columns + first * LANES, LANES)
        return jnp.dot(
            gathered[part][which], gate_up[pl.ds(start, count * LANES), :],
            preferred_element_type=jnp.float32,
        )

    def hidden_to(rows_half, ry, rx):
        ref = hidden.at[rows_half, chip]
        return remote(
            ref, ref, hidden_send.at[rows_half, ry * NX + rx],
            hidden_recv.at[rows_half, mirror[ry, rx]],
            CORES * chip_at(ry, rx) + core, ep,
        )

    def send_hidden(rows_half, both):
        parts = []
        for k in range(CORES):
            gate = both[:, 2 * k * units : (2 * k + 1) * units]
            upper = both[:, (2 * k + 1) * units : (2 * k + 2) * units]
            parts.append(gate / (1.0 + jnp.exp(-gate)) * upper)
        hidden[rows_half, chip] = jnp.concatenate(parts, axis=1).astype(jnp.bfloat16)
        for ry, rx in relative:
            hidden_to(rows_half, ry, rx).start()

    order = [(1, 0), (0, 1), (0, 3), (1, 1), (1, 3), (0, 2), (1, 2)]

    def lower(rows_half, part, ry, rx):
        which = chip_at(ry, rx)
        return jnp.dot(
            hidden[rows_half, which],
            downs[part][which].reshape(CORES * units, COLUMN_PARTS[part][1] * LANES),
            preferred_element_type=jnp.float32,
        )

    def send_back(rows_half, j, result):
        pieces = []
        for at in range(4):
            low, high = at * LANES, min((at + 1) * LANES, own)
            piece = result[:, low:high]
            if high - low < LANES:
                piece = jnp.concatenate(
                    [piece, jnp.zeros((span, LANES - (high - low)), jnp.float32)], axis=1
                )
            pieces.append(piece.reshape(NZ // 2, CAP, LANES))
        back_out[rows_half, j] = jnp.concatenate(pieces, axis=1).astype(jnp.bfloat16)
        apart = mod(parity + rows_half, 2)

        def send(steps):
            other = mod(z + 2 * steps + apart, NZ)
            remote(
                back_out.at[rows_half, j, quotient(other, 2)], back_in.at[core, z],
                back_sem.at[0], back_sem.at[1],
                CORES * chip + j, far_side * NZ + other,
            ).start()

        for i in range(1, NZ // 2):
            send(NZ // 4 + quotient(i, 2) * (1 - 2 * mod(i, 2)))

        @pl.when(apart == 1)
        def _():
            send(0)

    def finish(rows_half):
        low_part = lower(rows_half, 0, 0, 0)
        for ry, rx in order:
            hidden_to(rows_half, ry, (NX - rx) % NX).wait_recv()
            low_part += lower(rows_half, 0, ry, rx)
        send_back(rows_half, 0, low_part)
        high_part = lower(rows_half, 1, 0, 0)
        for ry, rx in order:
            high_part += lower(rows_half, 1, ry, rx)
        send_back(rows_half, 1, jnp.concatenate([low_part[:, own:], high_part], axis=1))

    both = [jnp.zeros((span, CORES * 2 * units), jnp.float32) for _ in range(2)]
    seen = set()
    for step, (part, ry, rx, piece) in enumerate(ARRIVALS):
        here = (ry, rx)
        if here == (0, 0):
            arrive(part)
            for target in (up, plus, minus) if part in Y_FIRST else (plus, minus, up):
                pass_on(part, here, target)
        else:
            take(part, ry, rx, piece)
            if part in Y_FIRST:
                if here == up:
                    pass_on(part, here, plus)
                    pass_on(part, here, minus)
            elif ry == 0 and rx == 2:
                pass_on(part, here, up, piece)
            if part in Y_FIRST or ry == 0:
                if rx == 3:
                    pass_on(part, here, plus, 0)
                elif rx == 1:
                    pass_on(part, here, minus, 1)
            if part not in Y_FIRST and ry == 0 and rx != 2:
                pass_on(part, here, up)
        if step == 0:
            loads[1].wait()
            gate_up_pair.wait_recv()
        if DOWN_FROM <= step < DOWN_FROM + len(relative):
            down_to(1, *relative[step - DOWN_FROM]).start()
        if (part, ry, rx) == (2, 0, 0):
            share_down(0)
        seen.add((part, ry, rx, piece))
        if piece is None or (part, ry, rx, 1 - piece) in seen:
            both[part // 2] += project(part, ry, rx)
        if step == FIRST_HIDDEN:
            send_hidden(0, both[0])
            share_down(1)
        if step == FIRST_RETURN:
            down_pair(0).wait_recv()
            down_pair(1).wait_recv()
            finish(0)
    send_hidden(1, both[1])
    finish(1)

    back_near_out = back_out.at[parity]
    back_zero = remote(
        back_near_out.at[0, quotient(z, 2)], back_in.at[core, z],
        back_near.at[0], back_near.at[2 + core], CORES * chip, far_side * NZ + z,
    )
    back_one = remote(
        back_near_out.at[1, quotient(z, 2)], back_in.at[core, z],
        back_near.at[1], back_near.at[2 + core], CORES * chip + 1, far_side * NZ + z,
    )
    back_one.start()

    @pl.when(core == 1)
    def _():
        back_zero.start()

    @pl.when(core == 0)
    def _():
        pltpu.make_async_copy(
            back_near_out.at[0, quotient(z, 2)], back_in.at[core, z], back_near.at[2 + core]
        ).start()

    most_pipe = pl.ds(0, PIPE - 1)
    pltpu.make_async_copy(score_in.at[most_pipe], score_in.at[most_pipe], score_sem.at[1]).wait()
    affinity = jax.nn.sigmoid(jnp.sum(score_in[...], axis=0))
    group, experts = affinity.shape
    pick_token = lax.broadcasted_iota(jnp.int32, (group, tok), 1)
    pick_row = lax.broadcasted_iota(jnp.int32, (group, tok), 0)
    pick = jnp.where(pick_token == pick_row + pipe * group, 1.0, 0.0).astype(jnp.bfloat16)
    chosen_all, _ = one_hot(names, 0, 1, experts)
    chosen = lax.dot_general(
        pick, chosen_all.astype(jnp.bfloat16), (((1,), (1,)), ((), ())),
        preferred_element_type=jnp.float32,
    )
    fraction = 2.5 * affinity / jnp.sum(chosen * affinity, axis=1, keepdims=True)
    spread_row = lax.broadcasted_iota(jnp.int32, (experts, total_slots), 0)
    spread_lane = lax.broadcasted_iota(jnp.int32, (experts, total_slots), 1)
    slot_expert = mod(spread_lane // CAP + side * NZ, HALVES * NZ)
    weight_out[...] = jnp.dot(
        fraction, jnp.where(spread_row == slot_expert, 1.0, 0.0),
        preferred_element_type=jnp.float32, precision=lax.Precision.HIGHEST,
    )
    weight_in[pipe] = weight_out[...]

    def send_weights(i, _):
        other = mod(pipe + i, PIPE)
        remote(weight_out, weight_in.at[pipe], weight_sem.at[0], weight_sem.at[1], other, ep).start()
        return 0

    lax.fori_loop(1, PIPE, send_weights, 0)

    slots_all = slot_matrix(names, 0, total_slots)
    slots_now = jnp.where(
        side == 0, slots_all, jnp.concatenate([slots_all[half:], slots_all[:half]], axis=0)
    )
    pltpu.make_async_copy(
        weight_in.at[most_pipe], weight_in.at[most_pipe], weight_sem.at[1]
    ).wait()
    combining = jnp.transpose(slots_now) * weight_in[...].reshape(tok, total_slots)
    chip_tokens = tokens[:, block].astype(jnp.float32)
    padding = jnp.zeros((tok, 4 * LANES - own), jnp.float32)
    residual = jnp.where(
        core == 0, chip_tokens[:, : 4 * LANES],
        jnp.concatenate([chip_tokens[:, own:], padding], axis=1),
    )

    rows_left(1)
    pltpu.make_async_copy(
        score_out.at[most_pipe], score_out.at[most_pipe], score_sem.at[0]
    ).wait()
    pltpu.make_async_copy(
        weight_in.at[most_pipe], weight_in.at[most_pipe], weight_sem.at[0]
    ).wait()
    for ry, rx in relative:
        down_to(0, ry, rx).wait_send()
        down_to(1, ry, rx).wait_send()
        hidden_to(0, ry, rx).wait_send()
        hidden_to(1, ry, rx).wait_send()
    for copy in sent:
        copy.wait_send()
    gate_up_pair.wait_send()
    down_pair(0).wait_send()
    down_pair(1).wait_send()

    pltpu.make_async_copy(
        back_in.at[:, most], back_in.at[:, most], back_sem.at[1]
    ).wait()
    for k in range(HALVES):
        pltpu.make_async_copy(back_in.at[k, 0], back_in.at[k, 0], back_near.at[2 + k]).wait()
    returned = back_in[...].astype(jnp.float32)
    returned = jnp.concatenate(
        [
            returned[:, :, at * CAP : (at + 1) * CAP, :].reshape(total_slots, LANES)
            for at in range(4)
        ],
        axis=1,
    )
    mixed = residual + jnp.dot(
        combining, returned, preferred_element_type=jnp.float32, precision=lax.Precision.HIGHEST
    )
    out_ref[...] = jnp.transpose(mixed)[:own, :].astype(jnp.bfloat16)

    @pl.when(core == 1)
    def _():
        back_zero.wait_send()

    back_one.wait_send()
    pltpu.make_async_copy(back_in.at[:, most], back_in.at[:, most], back_sem.at[0]).wait()


def shards(tokens, norm_gain, router, routes, w_gate_up, w_down):
    tok, width = tokens.shape
    columns = width // CHIPS
    half = NZ * CAP
    units = w_down.shape[1]
    experts = router.shape[1]
    group = tok // PIPE
    bf16, f32 = jnp.bfloat16, jnp.float32
    dma = pltpu.SemaphoreType.DMA
    anywhere = pl.BlockSpec(memory_space=pl.ANY)
    vmem = pl.BlockSpec(memory_space=pltpu.VMEM)
    mixed = pl.pallas_call(
        kernel,
        out_shape=jax.ShapeDtypeStruct((width // PIPE, tok), bf16),
        in_specs=[anywhere, vmem, anywhere, vmem, anywhere, anywhere],
        out_specs=vmem,
        scratch_shapes=[
            pltpu.VMEM((tok, width), bf16),
            pltpu.VMEM((columns, experts), bf16),
            pltpu.VMEM((width, CORES * 2 * units), bf16),
            *[
                pltpu.VMEM((CHIPS, CORES, units, count * LANES), bf16)
                for _, count in COLUMN_PARTS
            ],
            pltpu.VMEM((len(COLUMN_PARTS), NZ, PIECE, LANES), bf16),
            pltpu.VMEM((2, len(COLUMN_PARTS), NZ // 2, PIECE, LANES), bf16),
            *[pltpu.VMEM((CHIPS, half // 2, count * LANES), bf16) for _, _, count in PARTS],
            pltpu.VMEM((2, CHIPS, half // 2, CORES * units), bf16),
            pltpu.VMEM((2, CORES, NZ // 2, 32, LANES), bf16),
            pltpu.VMEM((HALVES, NZ, 32, LANES), bf16),
            pltpu.VMEM((PIPE, group, experts), f32),
            pltpu.VMEM((PIPE, group, experts), f32),
            pltpu.VMEM((group, 2 * half), f32),
            pltpu.VMEM((PIPE, group, 2 * half), f32),
            dma((8,)), dma((4,)), dma((6,)),
            dma((9 * len(PARTS),)), dma((2 * len(PARTS) * CHIPS,)), dma((6,)),
            dma((2, 2 * CHIPS)), dma((2, CHIPS)), dma((2, CHIPS)),
            dma((2,)), dma((4,)), dma((2,)), dma((2,)),
        ],
        compiler_params=pltpu.CompilerParams(
            collective_id=0, has_side_effects=True, vmem_limit_bytes=56 * 1024 * 1024
        ),
        cost_estimate=pl.CostEstimate(
            flops=2_000_000_000, bytes_accessed=8_000_000, transcendentals=100_000
        ),
    )(tokens, norm_gain.reshape(1, width), router, routes.T, w_gate_up, w_down)
    return mixed.T


def solution(mesh):
    placed = (
        P("ep", None),
        P(),
        P("pipe", None),
        P("ep", None),
        P("ep", None, "pipe"),
        P("ep", "pipe", None),
    )
    return jax.shard_map(
        shards, mesh=mesh, in_specs=placed, out_specs=P("ep", "pipe"), check_vma=False
    )
```

```python
import functools

import jax
import jax.numpy as jnp
from jax import lax
from jax.experimental import pallas as pl
from jax.experimental.pallas import tpu as pltpu
from jax.sharding import PartitionSpec as P

CORES = 2
NX = 4
NY = 2
CHIPS = NX * NY
PIPE = CHIPS * CORES
NZ = 16
HALVES = 2
CAP = 8
COLUMN_PARTS = ((0, 4), (4, 3))
PARTS = tuple((rows, first, count) for rows in (0, 1) for first, count in COLUMN_PARTS)
PIECE = 32
Y_FIRST = (1, 2)
ARRIVALS = (
    (0, 0, 0, None), (1, 0, 0, None), (0, 0, 3, None), (0, 0, 1, None), (0, 1, 0, None),
    (2, 0, 0, None), (1, 0, 3, None), (1, 0, 1, None), (1, 1, 0, None), (0, 0, 2, 0),
    (0, 0, 2, 1), (0, 1, 3, None), (3, 0, 0, None), (2, 0, 3, None), (2, 0, 1, None),
    (1, 0, 2, 0), (1, 0, 2, 1), (0, 1, 1, None), (1, 1, 3, None), (1, 1, 1, None),
    (2, 1, 0, None), (3, 0, 1, None), (0, 1, 2, 0), (2, 0, 2, 1), (0, 1, 2, 1),
    (3, 0, 3, None), (2, 0, 2, 0), (1, 1, 2, 0), (1, 1, 2, 1), (3, 1, 0, None),
    (2, 1, 3, None), (2, 1, 1, None), (3, 0, 2, 1), (3, 0, 2, 0), (2, 1, 2, 0),
    (2, 1, 2, 1), (3, 1, 1, None), (3, 1, 3, None), (3, 1, 2, 1), (3, 1, 2, 0),
)
DOWN_FROM, FIRST_HIDDEN, FIRST_RETURN = 9, 28, 33
LANES = 128
MESH = pl.DeviceIdType.MESH


def mod(value, size):
    return value & (size - 1)


def quotient(value, size):
    return value >> (size.bit_length() - 1)


def remote(src, dst, send, recv, pipe, ep):
    return pltpu.make_async_remote_copy(
        src_ref=src,
        dst_ref=dst,
        send_sem=send,
        recv_sem=recv,
        device_id=(pipe, ep),
        device_id_type=MESH,
    )


def one_hot(names, first, count, width):
    row = lax.broadcasted_iota(jnp.int32, (width, names.shape[1]), 0)
    expert = first + row // count
    named = names[0:1, :] == expert
    for k in range(1, names.shape[0]):
        named = named | (names[k : k + 1, :] == expert)
    return jnp.where(named, 1.0, 0.0), row


def slot_matrix(names, first, width):
    named, row = one_hot(names, first, CAP, width)
    tok = names.shape[1]
    earlier = lax.broadcasted_iota(jnp.int32, (tok, tok), 0) < lax.broadcasted_iota(
        jnp.int32, (tok, tok), 1
    )
    rank = jnp.dot(
        named.astype(jnp.bfloat16),
        jnp.where(earlier, 1.0, 0.0).astype(jnp.bfloat16),
        preferred_element_type=jnp.float32,
    )
    return jnp.where(rank == (row % CAP).astype(jnp.float32), named, 0.0)


def kernel(
    tokens_hbm, gain_ref, router_hbm, routes_ref, gate_up_hbm, down_hbm, out_ref,
    tokens, router, gate_up, down_a, down_b,
    outbox, inbox, rows_a, rows_b, rows_c, rows_d, hidden, back_out, back_in,
    score_out, score_in, weight_out, weight_in,
    load_sem, near_sem, out_sem, gather_send, gather_recv, pair_sem,
    down_sem, hidden_send, hidden_recv, back_sem, back_near,
    score_sem, weight_sem,
):
    pipe, ep = lax.axis_index("pipe"), lax.axis_index("ep")
    core, chip = mod(pipe, CORES), quotient(pipe, CORES)
    x, y = mod(chip, NX), quotient(chip, NX)
    z, side = mod(ep, NZ), quotient(ep, NZ)
    far_side = mod(side + core, HALVES)
    partner = pipe + 1 - 2 * core
    tok, width = tokens.shape
    columns = width // CHIPS
    tiles = columns // LANES
    half = NZ * CAP
    own = columns // CORES
    units = down_a.shape[2]
    parity = mod(z, 2)
    span = half // 2
    downs = (down_a, down_b)
    total_slots = HALVES * half

    def column_block(which):
        return pl.ds(pl.multiple_of(which * columns, LANES), columns)

    def down_columns(part, which):
        first, count = COLUMN_PARTS[part]
        start = pl.multiple_of(which * columns + first * LANES, LANES)
        return down_hbm.at[0, :, pl.ds(start, count * LANES)]

    def far_first(i):
        return mod(z + NZ // 2 + quotient(i, 2) * (1 - 2 * mod(i, 2)), NZ)

    own_lanes = pl.ds(pl.multiple_of(core * 2 * units, LANES), 2 * units)
    quarter = width // 4
    token_loads = [
        pltpu.make_async_copy(
            tokens_hbm.at[:, pl.ds(n * quarter, quarter)],
            tokens.at[:, pl.ds(n * quarter, quarter)],
            load_sem.at[4 + n],
        )
        for n in range(4)
    ]
    for load in token_loads:
        load.start()

    barrier = pltpu.get_barrier_semaphore()

    def greet_ep(i, _):
        other = far_first(i)
        for k in range(CORES):
            pl.semaphore_signal(
                barrier, inc=1,
                device_id=(CORES * chip + k, mod(side + k, HALVES) * NZ + other),
                device_id_type=MESH,
            )
        return 0

    lax.fori_loop(1, NZ, greet_ep, 0)
    pl.semaphore_signal(
        barrier, inc=1,
        device_id=(CORES * chip + 1, (1 - side) * NZ + z), device_id_type=MESH,
    )

    @pl.when(core == 1)
    def _():
        pl.semaphore_signal(barrier, inc=1, device_id=(partner, ep), device_id_type=MESH)

    def greet_pipe(i, _):
        pl.semaphore_signal(
            barrier, inc=1, device_id=(mod(pipe + i, PIPE), ep), device_id_type=MESH
        )
        return 0

    lax.fori_loop(1, PIPE, greet_pipe, 0)

    names = routes_ref[...]
    placing = slot_matrix(names, mod(core + side, HALVES) * NZ, half).astype(jnp.bfloat16)

    squares = jnp.zeros((tok, LANES), jnp.float32)
    for n in range(4):
        token_loads[n].wait()
        for at in range(n * quarter // LANES, (n + 1) * quarter // LANES):
            values = tokens[:, at * LANES : (at + 1) * LANES].astype(jnp.float32)
            squares += values * values
    router[...] = jnp.zeros_like(router)
    loads = [
        pltpu.make_async_copy(src, dst, load_sem.at[number])
        for number, (src, dst) in enumerate(
            ((router_hbm, router.at[pl.ds(core * own, own), :]),
             (gate_up_hbm.at[0], gate_up.at[:, own_lanes]),
             (down_columns(0, chip), down_a.at[chip, core]),
             (down_columns(1, chip), down_b.at[chip, core]))
        )
    ]
    for load in loads:
        load.start()
    scale = lax.rsqrt(jnp.sum(squares, axis=1, keepdims=True) / width + 1e-06)
    block = column_block(chip)
    normed = (tokens[:, block].astype(jnp.float32) * scale * gain_ref[:, block]).astype(
        jnp.bfloat16
    )
    placed = jnp.dot(placing, normed, preferred_element_type=jnp.float32)
    for part, (first, count) in enumerate(COLUMN_PARTS):
        pieces = [
            placed[:, at * LANES : (at + 1) * LANES].reshape(NZ, CAP, LANES)
            for at in range(first, first + count)
        ]
        if count * CAP < PIECE:
            pieces.append(jnp.zeros((NZ, PIECE - count * CAP, LANES), jnp.float32))
        outbox[part] = jnp.concatenate(pieces, axis=1).astype(jnp.bfloat16)

    pl.semaphore_wait(barrier, PIPE - 1 + 2 * NZ - 1 + core)

    def near_copy(part):
        return remote(
            outbox.at[part, z], inbox.at[parity, part, quotient(z, 2)],
            near_sem.at[part], near_sem.at[2 + part], pipe, far_side * NZ + z,
        )

    def send_rows(part):
        for i in range(1, NZ):
            other = far_first(i)
            remote(
                outbox.at[part, other], inbox.at[parity, part, quotient(z, 2)],
                out_sem.at[part], out_sem.at[2 + 2 * parity + part],
                pipe, far_side * NZ + other,
            ).start()

        @pl.when(core == 1)
        def _():
            near_copy(part).start()

        @pl.when(core == 0)
        def _():
            pltpu.make_async_copy(
                outbox.at[part, z], inbox.at[parity, part, quotient(z, 2)], near_sem.at[2 + part]
            ).start()

    def rows_left(part):
        pltpu.make_async_copy(
            outbox.at[part, most], outbox.at[part, most], out_sem.at[part]
        ).wait()

        @pl.when(core == 1)
        def _():
            near_copy(part).wait_send()

    most = pl.ds(0, NZ - 1)

    @pl.when(parity == 0)
    def _():
        send_rows(0)

    def chip_at(ry, rx):
        return mod(y + ry, NY) * NX + mod(x + rx, NX)

    relative = [(ry, rx) for rx in (2, 1, 3, 0) for ry in (1, 0) if (ry, rx) != (0, 0)]
    mirror = {(ry, rx): ry * NX + (NX - rx) % NX for ry, rx in relative}

    def down_to(part, ry, rx):
        return remote(
            down_columns(part, chip_at(ry, rx)), downs[part].at[chip, core],
            down_sem.at[part, ry * NX + rx], down_sem.at[part, CHIPS + mirror[ry, rx]],
            CORES * chip_at(ry, rx) + core, ep,
        )

    def down_pair(part):
        return remote(
            downs[part].at[:, core], downs[part].at[:, core],
            pair_sem.at[2 + 2 * part], pair_sem.at[3 + 2 * part], partner, ep,
        )

    def share_down(part):
        loads[2 + part].wait()
        for ry, rx in relative:
            down_to(part, ry, rx).wait_recv()
        down_pair(part).start()

    for ry, rx in relative:
        down_to(0, ry, rx).start()
    gate_up_pair = remote(
        gate_up_hbm.at[0], gate_up.at[:, own_lanes], pair_sem.at[0], pair_sem.at[1], partner, ep
    )
    gate_up_pair.start()

    loads[0].wait()
    scores = jnp.dot(normed, router[...], preferred_element_type=jnp.float32)
    score_out[...] = scores.reshape(score_out.shape)
    score_in[pipe] = score_out[pipe]

    def send_scores(i, _):
        other = mod(pipe + i, PIPE)
        remote(
            score_out.at[other], score_in.at[pipe], score_sem.at[0], score_sem.at[1], other, ep
        ).start()
        return 0

    lax.fori_loop(1, PIPE, send_scores, 0)

    @pl.when(parity == 0)
    def _():
        rows_left(0)
        send_rows(1)

    gathered = (rows_a, rows_b, rows_c, rows_d)
    sent = []

    def arrive(part):
        rows_half, _, count = PARTS[part]
        column_part = part % 2
        box = inbox.at[rows_half, column_part]
        others = box.at[pl.ds(0, NZ // 2 - 1)]

        @pl.when(parity == rows_half)
        def _():
            pltpu.make_async_copy(others, others, out_sem.at[2 + part]).wait()
            pltpu.make_async_copy(box.at[0], box.at[0], near_sem.at[2 + column_part]).wait()

        @pl.when(parity != rows_half)
        def _():
            pltpu.make_async_copy(box, box, out_sem.at[2 + part]).wait()
            if rows_half == 0:
                if column_part == 1:
                    rows_left(0)
                send_rows(column_part)

        arrived = inbox[rows_half, column_part].astype(jnp.float32)
        for at in range(count):
            gathered[part][chip, :, at * LANES : (at + 1) * LANES] = (
                arrived[:, at * CAP : (at + 1) * CAP, :].reshape(span, LANES).astype(jnp.bfloat16)
            )

    def block_ref(part, ry, rx, piece):
        ref = gathered[part].at[chip_at(ry, rx)]
        return ref if piece is None else ref.at[pl.ds(piece * (span // 2), span // 2), :]

    def recv_sem(part, ry, rx, piece):
        return gather_recv.at[(part * CHIPS + (ry % NY) * NX + rx % NX) * 2 + (piece or 0)]

    def pass_on(part, block, target, piece=None):
        (ry, rx), (ty, tx) = block, target
        ref = block_ref(part, ry, rx, piece)
        copy = remote(
            ref, ref, gather_send.at[len(sent)], recv_sem(part, ry + ty, rx - tx + NX, piece),
            CORES * chip_at(ty, tx) + core, ep,
        )
        copy.start()
        sent.append(copy)

    def take(part, ry, rx, piece=None):
        ref = block_ref(part, ry, rx, piece)
        pltpu.make_async_copy(ref, ref, recv_sem(part, ry, rx, piece)).wait()

    up, plus, minus = (1, 0), (0, 1), (0, 3)

    def project(part, ry, rx):
        _, first, count = PARTS[part]
        which = chip_at(ry, rx)
        start = pl.multiple_of(which * columns + first * LANES, LANES)
        return jnp.dot(
            gathered[part][which], gate_up[pl.ds(start, count * LANES), :],
            preferred_element_type=jnp.float32,
        )

    def hidden_to(rows_half, ry, rx):
        ref = hidden.at[rows_half, chip]
        return remote(
            ref, ref, hidden_send.at[rows_half, ry * NX + rx],
            hidden_recv.at[rows_half, mirror[ry, rx]],
            CORES * chip_at(ry, rx) + core, ep,
        )

    def send_hidden(rows_half, both):
        parts = []
        for k in range(CORES):
            gate = both[:, 2 * k * units : (2 * k + 1) * units]
            upper = both[:, (2 * k + 1) * units : (2 * k + 2) * units]
            parts.append(gate / (1.0 + jnp.exp(-gate)) * upper)
        hidden[rows_half, chip] = jnp.concatenate(parts, axis=1).astype(jnp.bfloat16)
        for ry, rx in relative:
            hidden_to(rows_half, ry, rx).start()

    order = [(1, 0), (0, 1), (0, 3), (1, 1), (1, 3), (0, 2), (1, 2)]

    def lower(rows_half, part, ry, rx):
        which = chip_at(ry, rx)
        return jnp.dot(
            hidden[rows_half, which],
            downs[part][which].reshape(CORES * units, COLUMN_PARTS[part][1] * LANES),
            preferred_element_type=jnp.float32,
        )

    def send_back(rows_half, j, result):
        pieces = []
        for at in range(4):
            low, high = at * LANES, min((at + 1) * LANES, own)
            piece = result[:, low:high]
            if high - low < LANES:
                piece = jnp.concatenate(
                    [piece, jnp.zeros((span, LANES - (high - low)), jnp.float32)], axis=1
                )
            pieces.append(piece.reshape(NZ // 2, CAP, LANES))
        back_out[rows_half, j] = jnp.concatenate(pieces, axis=1).astype(jnp.bfloat16)
        apart = mod(parity + rows_half, 2)

        def send(steps):
            other = mod(z + 2 * steps + apart, NZ)
            remote(
                back_out.at[rows_half, j, quotient(other, 2)], back_in.at[core, z],
                back_sem.at[0], back_sem.at[1],
                CORES * chip + j, far_side * NZ + other,
            ).start()

        for i in range(1, NZ // 2):
            send(NZ // 4 + quotient(i, 2) * (1 - 2 * mod(i, 2)))

        @pl.when(apart == 1)
        def _():
            send(0)

    def finish(rows_half):
        low_part = lower(rows_half, 0, 0, 0)
        for ry, rx in order:
            hidden_to(rows_half, ry, (NX - rx) % NX).wait_recv()
            low_part += lower(rows_half, 0, ry, rx)
        send_back(rows_half, 0, low_part)
        high_part = lower(rows_half, 1, 0, 0)
        for ry, rx in order:
            high_part += lower(rows_half, 1, ry, rx)
        send_back(rows_half, 1, jnp.concatenate([low_part[:, own:], high_part], axis=1))

    both = [jnp.zeros((span, CORES * 2 * units), jnp.float32) for _ in range(2)]
    seen = set()
    for step, (part, ry, rx, piece) in enumerate(ARRIVALS):
        here = (ry, rx)
        if here == (0, 0):
            arrive(part)
            for target in (up, plus, minus) if part in Y_FIRST else (plus, minus, up):
                pass_on(part, here, target)
        else:
            take(part, ry, rx, piece)
            if part in Y_FIRST:
                if here == up:
                    pass_on(part, here, plus)
                    pass_on(part, here, minus)
            elif ry == 0 and rx == 2:
                pass_on(part, here, up, piece)
            if part in Y_FIRST or ry == 0:
                if rx == 3:
                    pass_on(part, here, plus, 0)
                elif rx == 1:
                    pass_on(part, here, minus, 1)
            if part not in Y_FIRST and ry == 0 and rx != 2:
                pass_on(part, here, up)
        if step == 0:
            loads[1].wait()
            gate_up_pair.wait_recv()
        if DOWN_FROM <= step < DOWN_FROM + len(relative):
            down_to(1, *relative[step - DOWN_FROM]).start()
        if (part, ry, rx) == (2, 0, 0):
            share_down(0)
        seen.add((part, ry, rx, piece))
        if piece is None or (part, ry, rx, 1 - piece) in seen:
            both[part // 2] += project(part, ry, rx)
        if step == FIRST_HIDDEN:
            send_hidden(0, both[0])
            share_down(1)
        if step == FIRST_RETURN:
            down_pair(0).wait_recv()
            down_pair(1).wait_recv()
            finish(0)
    send_hidden(1, both[1])
    finish(1)

    back_near_out = back_out.at[parity]
    back_zero = remote(
        back_near_out.at[0, quotient(z, 2)], back_in.at[core, z],
        back_near.at[0], back_near.at[2 + core], CORES * chip, far_side * NZ + z,
    )
    back_one = remote(
        back_near_out.at[1, quotient(z, 2)], back_in.at[core, z],
        back_near.at[1], back_near.at[2 + core], CORES * chip + 1, far_side * NZ + z,
    )
    back_one.start()

    @pl.when(core == 1)
    def _():
        back_zero.start()

    @pl.when(core == 0)
    def _():
        pltpu.make_async_copy(
            back_near_out.at[0, quotient(z, 2)], back_in.at[core, z], back_near.at[2 + core]
        ).start()

    most_pipe = pl.ds(0, PIPE - 1)
    pltpu.make_async_copy(score_in.at[most_pipe], score_in.at[most_pipe], score_sem.at[1]).wait()
    affinity = jax.nn.sigmoid(jnp.sum(score_in[...], axis=0))
    group, experts = affinity.shape
    pick_token = lax.broadcasted_iota(jnp.int32, (group, tok), 1)
    pick_row = lax.broadcasted_iota(jnp.int32, (group, tok), 0)
    pick = jnp.where(pick_token == pick_row + pipe * group, 1.0, 0.0).astype(jnp.bfloat16)
    chosen_all, _ = one_hot(names, 0, 1, experts)
    chosen = lax.dot_general(
        pick, chosen_all.astype(jnp.bfloat16), (((1,), (1,)), ((), ())),
        preferred_element_type=jnp.float32,
    )
    fraction = 2.5 * affinity / jnp.sum(chosen * affinity, axis=1, keepdims=True)
    spread_row = lax.broadcasted_iota(jnp.int32, (experts, total_slots), 0)
    spread_lane = lax.broadcasted_iota(jnp.int32, (experts, total_slots), 1)
    slot_expert = mod(spread_lane // CAP + side * NZ, HALVES * NZ)
    weight_out[...] = jnp.dot(
        fraction, jnp.where(spread_row == slot_expert, 1.0, 0.0),
        preferred_element_type=jnp.float32, precision=lax.Precision.HIGHEST,
    )
    weight_in[pipe] = weight_out[...]

    def send_weights(i, _):
        other = mod(pipe + i, PIPE)
        remote(weight_out, weight_in.at[pipe], weight_sem.at[0], weight_sem.at[1], other, ep).start()
        return 0

    lax.fori_loop(1, PIPE, send_weights, 0)

    slots_all = slot_matrix(names, 0, total_slots)
    slots_now = jnp.where(
        side == 0, slots_all, jnp.concatenate([slots_all[half:], slots_all[:half]], axis=0)
    )
    pltpu.make_async_copy(
        weight_in.at[most_pipe], weight_in.at[most_pipe], weight_sem.at[1]
    ).wait()
    combining = jnp.transpose(slots_now) * weight_in[...].reshape(tok, total_slots)
    chip_tokens = tokens[:, block].astype(jnp.float32)
    padding = jnp.zeros((tok, 4 * LANES - own), jnp.float32)
    residual = jnp.where(
        core == 0, chip_tokens[:, : 4 * LANES],
        jnp.concatenate([chip_tokens[:, own:], padding], axis=1),
    )

    rows_left(1)
    pltpu.make_async_copy(
        score_out.at[most_pipe], score_out.at[most_pipe], score_sem.at[0]
    ).wait()
    pltpu.make_async_copy(
        weight_in.at[most_pipe], weight_in.at[most_pipe], weight_sem.at[0]
    ).wait()
    for ry, rx in relative:
        down_to(0, ry, rx).wait_send()
        down_to(1, ry, rx).wait_send()
        hidden_to(0, ry, rx).wait_send()
        hidden_to(1, ry, rx).wait_send()
    for copy in sent:
        copy.wait_send()
    gate_up_pair.wait_send()
    down_pair(0).wait_send()
    down_pair(1).wait_send()

    pltpu.make_async_copy(
        back_in.at[:, most], back_in.at[:, most], back_sem.at[1]
    ).wait()
    for k in range(HALVES):
        pltpu.make_async_copy(back_in.at[k, 0], back_in.at[k, 0], back_near.at[2 + k]).wait()
    returned = back_in[...].astype(jnp.float32)
    returned = jnp.concatenate(
        [
            returned[:, :, at * CAP : (at + 1) * CAP, :].reshape(total_slots, LANES)
            for at in range(4)
        ],
        axis=1,
    )
    mixed = residual + jnp.dot(
        combining, returned, preferred_element_type=jnp.float32, precision=lax.Precision.HIGHEST
    )
    out_ref[...] = jnp.transpose(mixed)[:own, :].astype(jnp.bfloat16)

    @pl.when(core == 1)
    def _():
        back_zero.wait_send()

    back_one.wait_send()
    pltpu.make_async_copy(back_in.at[:, most], back_in.at[:, most], back_sem.at[0]).wait()


def shards(tokens, norm_gain, router, routes, w_gate_up, w_down):
    tok, width = tokens.shape
    columns = width // CHIPS
    half = NZ * CAP
    units = w_down.shape[1]
    experts = router.shape[1]
    group = tok // PIPE
    bf16, f32 = jnp.bfloat16, jnp.float32
    dma = pltpu.SemaphoreType.DMA
    anywhere = pl.BlockSpec(memory_space=pl.ANY)
    vmem = pl.BlockSpec(memory_space=pltpu.VMEM)
    mixed = pl.pallas_call(
        kernel,
        out_shape=jax.ShapeDtypeStruct((width // PIPE, tok), bf16),
        in_specs=[anywhere, vmem, anywhere, vmem, anywhere, anywhere],
        out_specs=vmem,
        scratch_shapes=[
            pltpu.VMEM((tok, width), bf16),
            pltpu.VMEM((columns, experts), bf16),
            pltpu.VMEM((width, CORES * 2 * units), bf16),
            *[
                pltpu.VMEM((CHIPS, CORES, units, count * LANES), bf16)
                for _, count in COLUMN_PARTS
            ],
            pltpu.VMEM((len(COLUMN_PARTS), NZ, PIECE, LANES), bf16),
            pltpu.VMEM((2, len(COLUMN_PARTS), NZ // 2, PIECE, LANES), bf16),
            *[pltpu.VMEM((CHIPS, half // 2, count * LANES), bf16) for _, _, count in PARTS],
            pltpu.VMEM((2, CHIPS, half // 2, CORES * units), bf16),
            pltpu.VMEM((2, CORES, NZ // 2, 32, LANES), bf16),
            pltpu.VMEM((HALVES, NZ, 32, LANES), bf16),
            pltpu.VMEM((PIPE, group, experts), f32),
            pltpu.VMEM((PIPE, group, experts), f32),
            pltpu.VMEM((group, 2 * half), f32),
            pltpu.VMEM((PIPE, group, 2 * half), f32),
            dma((8,)), dma((4,)), dma((6,)),
            dma((9 * len(PARTS),)), dma((2 * len(PARTS) * CHIPS,)), dma((6,)),
            dma((2, 2 * CHIPS)), dma((2, CHIPS)), dma((2, CHIPS)),
            dma((2,)), dma((4,)), dma((2,)), dma((2,)),
        ],
        compiler_params=pltpu.CompilerParams(
            collective_id=0, has_side_effects=True, vmem_limit_bytes=56 * 1024 * 1024
        ),
        cost_estimate=pl.CostEstimate(
            flops=2_000_000_000, bytes_accessed=8_000_000, transcendentals=100_000
        ),
    )(tokens, norm_gain.reshape(1, width), router, routes.T, w_gate_up, w_down)
    return mixed.T


def solution(mesh):
    placed = (
        P("ep", None),
        P(),
        P("pipe", None),
        P("ep", None),
        P("ep", None, "pipe"),
        P("ep", "pipe", None),
    )
    return jax.shard_map(
        shards, mesh=mesh, in_specs=placed, out_specs=P("ep", "pipe"), check_vma=False
    )
```
